256 devices in a mesh: row: 16 (over z_lo, x, core), col: 16 (over z_hi, y).
Axes of the slice: x: 4, y: 4, z: 8 (z_hi: 4, z_lo: 2; z = z_hi * 2 + z_lo), core: 2. Of those that a mesh axis runs over, the one named last changes fastest.
Arguments:
- gate_pre: bfloat16 [2048, 26624], P('col', 'row'), may hold values from -6 to 6
- up_pre: bfloat16 [2048, 26624], P('col', 'row'), may hold values from -6 to 6
- down_weight: bfloat16 [26624, 16384], P('row', 'col'), may hold values from -0.0390625 to 0.0390625
- out_grad: bfloat16 [2048, 16384], P('row', 'col'), may hold values from -6 to 6
Outputs:
- ffn_out: bfloat16 [2048, 16384], P('row', 'col')
- gate_grad: bfloat16 [2048, 26624], P('col', 'row')
- up_grad: bfloat16 [2048, 26624], P('col', 'row')
The draws below stay inside these ranges and needn't reach their ends.
All inputs are finite; a program needn't handle non-finite values.
Results may differ from the reference program's by a relative error of at most 0.025.
Values may be sent and summed in bfloat16 or wider, within the bound.
A program may use at most 128 MiB of HBM per device.

```python
import jax
import jax.numpy as jnp
from jax import lax

D = 16384
FFW = 26624
TOKENS = 2048
N_ROW = 16
N_COL = 16


def raised(result, stream_key, source, target, blocks, factor):
    owner, partner = [(jnp.arange(result.shape[position]) // (result.shape[position] // blocks)).reshape([-1 if axis == position else 1 for axis in range(result.ndim)]) for position in (source, target)]
    chosen = jax.random.permutation(stream_key, blocks)[partner]
    strong = (owner == chosen) | (owner == (partner + blocks // 2) % blocks)
    return jnp.where(strong, factor * result, result)


def block_levels(rng, extent, cuts, least, top_value):
    def one(dim, parts):
        heights = jax.random.uniform(jax.random.fold_in(jax.random.fold_in(rng, 6), dim), (parts,), jnp.float32, least / len(cuts), top_value / len(cuts))
        return jnp.repeat(jnp.exp(heights), extent[dim] // parts).reshape((-1,) + (1,) * (len(extent) - dim - 1))

    gain = one(*cuts[0])
    for cut in cuts[1:]:
        gain = gain * one(*cut)
    return gain


def bell_draw(rng, shape, scale, limit, pieces=(), kind=jnp.bfloat16):
    result = scale * jax.random.normal(rng, shape, jnp.float32)
    if pieces:
        result = result * block_levels(rng, shape, pieces, -0.22, 0.18)
    return jnp.clip(result, -limit, limit).astype(kind)


def noise_with(key, dims, scale, reach, shards, heavy, kind=jnp.bfloat16):
    array = scale * jax.random.normal(key, dims, jnp.float32)
    if shards:
        array = array * block_levels(key, dims, shards, -0.22, 0.18)
    return jnp.clip(raised(array, jax.random.fold_in(key, 3), *heavy), -reach, reach).astype(kind)


def setup_inputs(seed: int = 0) -> dict:
    splits = jax.random.split(jax.random.key(seed), 5)
    gate_pre = noise_with(splits[0], (TOKENS, FFW), 1.0, 6.0, ((0, 16), (1, 16)), (1, 0, 16, 2.0))
    up_pre = bell_draw(splits[1], (TOKENS, FFW), 1.0, 6.0, ((0, 16), (1, 16)))
    down_weight = bell_draw(splits[2], (FFW, D), FFW ** -0.5, 0.0390625, ((0, 16), (1, 16)))
    out_grad = noise_with(splits[3], (TOKENS, D), 1.0, 6.0, ((0, 16), (1, 16)), (1, 0, 16, 2.0))
    return {"gate_pre": gate_pre, "up_pre": up_pre, "down_weight": down_weight, "out_grad": out_grad}


def reference(gate_pre, up_pre, down_weight, out_grad):
    gate_value = gate_pre.astype(jnp.float32)
    up_value = up_pre.astype(jnp.float32)
    hidden = (jax.nn.silu(gate_value) * up_value).astype(jnp.bfloat16)
    token_count = hidden.shape[0]
    hid_width = FFW // N_ROW
    feat_width = D // N_COL
    hidden_blocks = hidden.reshape(token_count, N_ROW, hid_width).transpose(1, 0, 2)
    weight_rows = down_weight.reshape(N_ROW, hid_width, D)

    def add_forward(running, pair):
        product = jnp.dot(pair[0], pair[1], preferred_element_type=jnp.float32).astype(jnp.bfloat16)
        product = lax.optimization_barrier(product)
        return running + product.astype(jnp.float32), None

    summed, _ = lax.scan(add_forward, jnp.zeros((token_count, D), jnp.float32), (hidden_blocks, weight_rows))
    ffn_out = summed.astype(jnp.bfloat16)

    grad_blocks = out_grad.reshape(token_count, N_COL, feat_width).transpose(1, 0, 2)
    weight_cols = down_weight.reshape(FFW, N_COL, feat_width).transpose(1, 0, 2)

    def add_backward(running, pair):
        product = lax.dot_general(pair[0], pair[1], (((1,), (1,)), ((), ())), preferred_element_type=jnp.float32).astype(jnp.bfloat16)
        product = lax.optimization_barrier(product)
        return running + product.astype(jnp.float32), None

    hidden_grad, _ = lax.scan(add_backward, jnp.zeros((token_count, FFW), jnp.float32), (grad_blocks, weight_cols))
    sigma = jax.nn.sigmoid(gate_value)
    gate_grad = (hidden_grad * up_value * sigma * (1.0 + gate_value * (1.0 - sigma))).astype(jnp.bfloat16)
    up_grad = (hidden_grad * gate_value * sigma).astype(jnp.bfloat16)
    return ffn_out, gate_grad, up_grad
```

```python
import jax
import jax.numpy as jnp
from jax import lax
from jax.sharding import PartitionSpec as P


def hidden_of(gate_part, up_part):
    gate_value = gate_part.astype(jnp.float32)
    return (jax.nn.silu(gate_value) * up_part.astype(jnp.float32)).astype(jnp.bfloat16)


def local(gate_pre, up_pre, down_weight, out_grad):
    hidden = lax.all_gather(hidden_of(gate_pre, up_pre), "col", axis=0, tiled=True)
    partial_out = jnp.dot(hidden, down_weight, preferred_element_type=jnp.float32)
    ffn_out = lax.psum_scatter(
        partial_out.astype(jnp.bfloat16), "row", scatter_dimension=0, tiled=True
    )
    partial_grad = lax.dot_general(
        lax.all_gather(out_grad, "row", axis=0, tiled=True),
        down_weight,
        (((1,), (1,)), ((), ())),
        preferred_element_type=jnp.float32,
    )
    hidden_grad = lax.psum_scatter(
        partial_grad.astype(jnp.bfloat16), "col", scatter_dimension=0, tiled=True
    ).astype(jnp.float32)
    gate_value = gate_pre.astype(jnp.float32)
    up_value = up_pre.astype(jnp.float32)
    sigma = jax.nn.sigmoid(gate_value)
    gate_grad = (hidden_grad * up_value * sigma * (1.0 + gate_value * (1.0 - sigma))).astype(
        jnp.bfloat16
    )
    up_grad = (hidden_grad * gate_value * sigma).astype(jnp.bfloat16)
    return (ffn_out, gate_grad, up_grad)


def solution(mesh):
    return jax.shard_map(
        local,
        mesh=mesh,
        in_specs=(P("col", "row"), P("col", "row"), P("row", "col"), P("row", "col")),
        out_specs=(P("row", "col"), P("col", "row"), P("col", "row")),
        check_vma=False,
    )
```

```python
import functools

import jax
import jax.numpy as jnp
from jax import lax
from jax.experimental import pallas as pl
from jax.experimental.pallas import tpu as pltpu
from jax.sharding import PartitionSpec as P

BF16, F32 = jnp.bfloat16, jnp.float32

Z_FIRST = 1408

MESSAGES = (
    ["g_z"]
    + [f"g_{what}{k}" for k in range(2) for what in ("xp", "xm", "hp", "hm", "s", "sp", "sm", "sf")]
    + ["h_zp", "h_zm", "h_zhp", "h_zhm", "q_yp", "q_ym", "q_yhp", "q_yhm", "q_zp", "q_zm", "q_zhp", "q_zhm"]
    + [f"h_{what}{k}" for k in range(4) for what in ("yp", "ym", "yhp", "yhm")]
    + [f"p_{what}{k}" for k in range(4) for what in ("yp", "ym", "yhp", "yhm")]
    + ["p_zp", "p_zm", "p_zhp", "p_zhm", "r_yp", "r_ym", "r_yhp", "r_yhm", "r_zp", "r_zm", "r_zhp", "r_zhm"]
    + [f"o_d{k}" for k in range(4)]
    + [f"o_{what}{m}" for m in range(2) for what in ("xp", "xm", "hp", "hm")]
    + ["o_z"]
)
NUMBER = {name: number for number, name in enumerate(MESSAGES)}


def kernel(
    gate, up, weight, cot, out, gate_grad, up_grad,
    hid, cots, part_out, part_grad,
    from_sib, x_full, x_half, x_sum, zl_in,
    y_full, y_half, y_sum, z_full, z_half,
    qz_full, qz_half, q_sum, qy_full, qy_half,
    send_sems, recv_sems,
):
    tokens, units = gate.shape
    feats = cot.shape[1]
    half = tokens // 2
    A, B, ALL = pl.ds(0, half), pl.ds(half, half), pl.ds(0, tokens)
    first = Z_FIRST
    FIRST, REST = pl.ds(0, first), pl.ds(first, units - first)

    row, col = lax.axis_index("row"), lax.axis_index("col")
    zl, x, core = row // 8, (row // 2) % 4, row % 2
    z, y = col // 4, col % 4
    xp, xm, xf = (x + 1) % 4, (x + 3) % 4, (x + 2) % 4
    yp, ym, yf = (y + 1) % 4, (y + 3) % 4, (y + 2) % 4
    zp, zm, zf = (z + 1) % 4, (z + 3) % 4, (z + 2) % 4

    def at_row(zl_, x_, core_):
        return zl_ * 8 + x_ * 2 + core_

    def at_col(z_, y_):
        return z_ * 4 + y_

    near = {
        "xp": {"row": at_row(zl, xp, core)},
        "xm": {"row": at_row(zl, xm, core)},
        "zl": {"row": at_row(1 - zl, x, core)},
        "sib": {"row": at_row(zl, x, 1 - core)},
        "yp": {"col": at_col(z, yp)},
        "ym": {"col": at_col(z, ym)},
        "zp": {"col": at_col(zp, y)},
        "zm": {"col": at_col(zm, y)},
    }

    sent = []

    def copy(name, src, dst, to):
        number = NUMBER[name]
        return pltpu.make_async_remote_copy(
            src_ref=src,
            dst_ref=dst,
            send_sem=send_sems.at[number],
            recv_sem=recv_sems.at[number],
            device_id=near[to],
            device_id_type=pl.DeviceIdType.MESH,
        )

    def send(name, src, dst, to):
        one = copy(name, src, dst, to)
        one.start()
        sent.append(one)

    def arrived(name, ref):
        copy(name, ref, ref, "sib").wait_recv()

    def chunks(count, body):
        def step(i, carry):
            body(pl.ds(pl.multiple_of(i * 16, 16), 16))
            return carry

        lax.fori_loop(0, count // 16, step, 0)

    def wide(ref):
        return ref[...].astype(F32)

    def add_into(ref, other):
        lead = (slice(None),) * (len(ref.shape) - 2)

        def body(rows):
            index = lead + (rows,)
            ref[index] = (ref[index].astype(F32) + other[index].astype(F32)).astype(BF16)

        chunks(ref.shape[-2], body)

    def sum_to(ref, terms):
        lead = (slice(None),) * (len(ref.shape) - 2)

        def body(rows):
            index = lead + (rows,)
            total = terms[0][index].astype(F32)
            for term in terms[1:]:
                total = total + term[index].astype(F32)
            ref[index] = total.astype(BF16)

        chunks(ref.shape[-2], body)

    barrier = pltpu.get_barrier_semaphore()
    for to in near.values():
        pl.semaphore_signal(barrier, inc=1, device_id=to, device_id_type=pl.DeviceIdType.MESH)

    cots[row] = cot[...]

    def make_hidden(rows):
        value = gate[rows].astype(F32)
        silu = value / (1.0 + jnp.exp(-value))
        hid[col, rows] = (silu * up[rows].astype(F32)).astype(BF16)

    chunks(tokens, make_hidden)
    pl.semaphore_wait(barrier, len(near))

    zls = (zl, 1 - zl)

    def g_block(k, x_, core_=core):
        return cots.at[at_row(zls[k], x_, core_)]

    def g_spread(k):
        send(f"g_xp{k}", g_block(k, x), g_block(k, x), "xp")
        send(f"g_xm{k}", g_block(k, x), g_block(k, x), "xm")
        send(f"g_s{k}", g_block(k, x), g_block(k, x), "sib")

    def g_relay(k):
        arrived(f"g_xp{k}", g_block(k, xm))
        send(f"g_hp{k}", g_block(k, xm).at[A], g_block(k, xm).at[A], "xp")
        arrived(f"g_xm{k}", g_block(k, xp))
        send(f"g_hm{k}", g_block(k, xp).at[B], g_block(k, xp).at[B], "xm")
        send(f"g_sm{k}", g_block(k, xm), g_block(k, xm), "sib")
        send(f"g_sp{k}", g_block(k, xp), g_block(k, xp), "sib")

    def g_far(k):
        arrived(f"g_hp{k}", g_block(k, xf).at[A])
        arrived(f"g_hm{k}", g_block(k, xf).at[B])
        send(f"g_sf{k}", g_block(k, xf), g_block(k, xf), "sib")

    def g_end(k):
        for what, x_ in (("s", x), ("sm", xm), ("sp", xp), ("sf", xf)):
            arrived(f"g_{what}{k}", g_block(k, x_, 1 - core))

    zs = (z, zm, zp, zf)

    def h_block(z_, y_, rows=ALL):
        return hid.at[at_col(z_, y_), rows, FIRST]

    def q_block(y_, rows=ALL):
        return hid.at[at_col(z, y_), rows, REST]

    def q_four(z_, rows=ALL):
        return hid.at[pl.ds(z_ * 4, 4), rows, REST]

    def h_spread(k):
        block = h_block(zs[k], y)
        send(f"h_yp{k}", block, block, "yp")
        send(f"h_ym{k}", block, block, "ym")

    def h_relay(k):
        arrived(f"h_yp{k}", h_block(zs[k], ym))
        block = h_block(zs[k], ym, A)
        send(f"h_yhp{k}", block, block, "yp")
        arrived(f"h_ym{k}", h_block(zs[k], yp))
        block = h_block(zs[k], yp, B)
        send(f"h_yhm{k}", block, block, "ym")

    def h_far(k):
        arrived(f"h_yhp{k}", h_block(zs[k], yf, A))
        arrived(f"h_yhm{k}", h_block(zs[k], yf, B))

    def q_y_relay():
        arrived("q_yp", q_block(ym))
        send("q_yhp", q_block(ym, A), q_block(ym, A), "yp")
        arrived("q_ym", q_block(yp))
        send("q_yhm", q_block(yp, B), q_block(yp, B), "ym")

    def q_z_spread():
        arrived("q_yhp", q_block(yf, A))
        arrived("q_yhm", q_block(yf, B))
        send("q_zp", q_four(z), q_four(z), "zp")
        send("q_zm", q_four(z), q_four(z), "zm")

    def h_z_relay():
        arrived("h_zp", h_block(zm, y))
        send("h_zhp", h_block(zm, y, A), h_block(zm, y, A), "zp")
        arrived("h_zm", h_block(zp, y))
        send("h_zhm", h_block(zp, y, B), h_block(zp, y, B), "zm")

    def q_z_relay():
        arrived("q_zp", q_four(zm))
        send("q_zhp", q_four(zm, A), q_four(zm, A), "zp")
        arrived("q_zm", q_four(zp))
        send("q_zhm", q_four(zp, B), q_four(zp, B), "zm")

    def q_z_far():
        arrived("q_zhp", q_four(zf, A))
        arrived("q_zhm", q_four(zf, B))

    def backward(z_):
        four = pl.ds(z_ * 4, 4)

        def tile(start, width):
            left = cots[four].reshape(4 * tokens, feats)
            product = lax.dot_general(
                left, weight[pl.ds(start, width)], (((1,), (1,)), ((), ())), preferred_element_type=F32
            )
            part_grad[four, :, pl.ds(start, width)] = product.astype(BF16).reshape(4, tokens, width)

        def step(i, carry):
            tile(pl.multiple_of(i * 256, 256), 256)
            return carry

        lax.fori_loop(0, units // 256, step, 0)
        if units % 256:
            tile(units // 256 * 256, units % 256)

    def forward(z_):
        four = pl.ds(z_ * 4, 4)

        def step(i, carry):
            columns = pl.ds(pl.multiple_of(i * 256, 256), 256)
            left = hid[four].reshape(4 * tokens, units)
            product = jnp.dot(left, weight[:, columns], preferred_element_type=F32).astype(BF16)
            for j in range(4):
                part_out[j % 2, z_ * 2 + j // 2, :, columns] = product[j * tokens : (j + 1) * tokens]
            return carry

        lax.fori_loop(0, feats // 256, step, 0)

    def pg(z_, y_, rows=ALL):
        return part_grad.at[at_col(z_, y_), rows, FIRST]

    def pq(z_, rows=ALL):
        return part_grad.at[pl.ds(z_ * 4, 4), rows, REST]

    def p_start(k):
        send(f"p_yhp{k}", pg(zs[k], yf, A), y_half.at[0, k], "yp")
        send(f"p_yhm{k}", pg(zs[k], yf, B), y_half.at[1, k], "ym")

    def p_relay(k):
        arrived(f"p_yhp{k}", y_half.at[0, k])
        add_into(pg(zs[k], yp, A), y_half.at[0, k])
        send(f"p_yp{k}", pg(zs[k], yp), y_full.at[0, k], "yp")
        arrived(f"p_yhm{k}", y_half.at[1, k])
        add_into(pg(zs[k], ym, B), y_half.at[1, k])
        send(f"p_ym{k}", pg(zs[k], ym), y_full.at[1, k], "ym")

    def p_here(k):
        arrived(f"p_yp{k}", y_full.at[0, k])
        arrived(f"p_ym{k}", y_full.at[1, k])
        if k:
            sum_to(y_sum.at[k - 1], (pg(zs[k], y), y_full.at[0, k], y_full.at[1, k]))

    def p_z_start():
        send("p_zhp", y_sum.at[2, A], z_half.at[0], "zp")
        send("p_zhm", y_sum.at[2, B], z_half.at[1], "zm")

    def p_z_relay():
        arrived("p_zhp", z_half.at[0])
        add_into(y_sum.at[1, A], z_half.at[0])
        send("p_zp", y_sum.at[1], z_full.at[0], "zp")
        arrived("p_zhm", z_half.at[1])
        add_into(y_sum.at[0, B], z_half.at[1])
        send("p_zm", y_sum.at[0], z_full.at[1], "zm")

    def r_z_start():
        send("r_zhp", pq(zf, A), qz_half.at[0], "zp")
        send("r_zhm", pq(zf, B), qz_half.at[1], "zm")

    def r_z_relay():
        arrived("r_zhp", qz_half.at[0])
        add_into(pq(zp, A), qz_half.at[0])
        send("r_zp", pq(zp), qz_full.at[0], "zp")
        arrived("r_zhm", qz_half.at[1])
        add_into(pq(zm, B), qz_half.at[1])
        send("r_zm", pq(zm), qz_full.at[1], "zm")

    def r_y_start():
        arrived("r_zp", qz_full.at[0])
        arrived("r_zm", qz_full.at[1])
        sum_to(q_sum, (pq(z), qz_full.at[0], qz_full.at[1]))
        send("r_yhp", q_sum.at[yf, A], qy_half.at[0], "yp")
        send("r_yhm", q_sum.at[yf, B], qy_half.at[1], "ym")

    def r_y_relay():
        arrived("r_yhp", qy_half.at[0])
        add_into(q_sum.at[yp, A], qy_half.at[0])
        send("r_yp", q_sum.at[yp], qy_full.at[0], "yp")
        arrived("r_yhm", qy_half.at[1])
        add_into(q_sum.at[ym, B], qy_half.at[1])
        send("r_ym", q_sum.at[ym], qy_full.at[1], "ym")

    def o_swap(k, z_):
        chips = pl.ds(z_ * 2, 2)
        send(f"o_d{k}", part_out.at[1 - core, chips], from_sib.at[chips], "sib")

    def o_pair(k, z_):
        chips = pl.ds(z_ * 2, 2)
        arrived(f"o_d{k}", from_sib.at[chips])
        add_into(part_out.at[core, chips], from_sib.at[chips])

    o_zls = (z // 2, 1 - z // 2)

    def o_block(m, x_, rows=ALL):
        return part_out.at[core, o_zls[m] * 4 + x_, rows]

    def o_start(m):
        send(f"o_hp{m}", o_block(m, xf, A), x_half.at[0, m], "xp")
        send(f"o_hm{m}", o_block(m, xf, B), x_half.at[1, m], "xm")

    def o_relay(m):
        arrived(f"o_hp{m}", x_half.at[0, m])
        add_into(o_block(m, xp, A), x_half.at[0, m])
        send(f"o_xp{m}", o_block(m, xp), x_full.at[0, m], "xp")
        arrived(f"o_hm{m}", x_half.at[1, m])
        add_into(o_block(m, xm, B), x_half.at[1, m])
        send(f"o_xm{m}", o_block(m, xm), x_full.at[1, m], "xm")

    def o_here(m):
        arrived(f"o_xp{m}", x_full.at[0, m])
        arrived(f"o_xm{m}", x_full.at[1, m])
        sum_to(x_sum.at[o_zls[m]], (o_block(m, x), x_full.at[0, m], x_full.at[1, m]))

    def o_end():
        arrived("o_z", zl_in)

        def body(rows):
            out[rows] = (x_sum[zl, rows].astype(F32) + zl_in[rows].astype(F32)).astype(BF16)

        chunks(tokens, body)

    send("g_z", g_block(0, x), g_block(0, x), "zl")
    g_spread(0)
    send("q_yp", q_block(y), q_block(y), "yp")
    send("q_ym", q_block(y), q_block(y), "ym")
    send("h_zp", h_block(z, y), h_block(z, y), "zp")
    send("h_zm", h_block(z, y), h_block(z, y), "zm")
    h_spread(0)
    q_y_relay()
    arrived("g_z", g_block(1, x))
    g_spread(1)
    g_relay(0)
    q_z_spread()
    h_relay(0)
    h_z_relay()
    h_spread(1)
    h_spread(2)
    g_relay(1)
    g_far(0)
    h_far(0)
    g_far(1)
    g_end(0)
    g_end(1)
    backward(zf)
    p_start(3)
    q_z_relay()
    arrived("h_zhp", h_block(zf, y, A))
    arrived("h_zhm", h_block(zf, y, B))
    h_spread(3)
    h_relay(1)
    h_relay(2)
    backward(zm)
    p_start(1)
    p_relay(3)
    backward(zp)
    p_start(2)
    r_z_start()
    h_relay(3)
    backward(z)
    p_start(0)
    p_relay(1)
    p_relay(2)
    p_here(3)
    p_z_start()
    p_relay(0)
    r_z_relay()
    q_z_far()
    forward(z)
    o_swap(0, z)
    h_far(1)
    h_far(2)
    pair = z + 1 - 2 * (z % 2)
    other = zp + zm - pair
    forward(pair)
    o_swap(1, pair)
    o_pair(0, z)
    forward(other)
    o_swap(2, other)
    o_pair(1, pair)
    o_start(0)
    h_far(3)
    forward(zf)
    o_swap(3, zf)
    o_pair(2, other)
    o_relay(0)
    p_here(1)
    p_here(2)
    p_z_relay()
    o_pair(3, zf)
    o_start(1)
    r_y_start()
    o_here(0)
    o_relay(1)
    r_y_relay()
    o_here(1)
    send("o_z", x_sum.at[1 - zl], zl_in, "zl")
    p_here(0)
    o_end()
    arrived("p_zp", z_full.at[0])
    arrived("p_zm", z_full.at[1])
    arrived("r_yp", qy_full.at[0])
    arrived("r_ym", qy_full.at[1])

    def finish(rows, columns, terms):
        grad = terms[0].astype(F32)
        for term in terms[1:]:
            grad = grad + term.astype(F32)
        gate_value = gate[rows, columns].astype(F32)
        up_value = up[rows, columns].astype(F32)
        sigma = 1.0 / (1.0 + jnp.exp(-gate_value))
        scaled = grad * sigma
        gate_grad[rows, columns] = (scaled * up_value * (1.0 + gate_value * (1.0 - sigma))).astype(BF16)
        up_grad[rows, columns] = (scaled * gate_value).astype(BF16)

    def last(rows):
        finish(
            rows,
            FIRST,
            (
                part_grad[col, rows, FIRST],
                y_full[0, 0, rows],
                y_full[1, 0, rows],
                z_full[0, rows],
                z_full[1, rows],
            ),
        )
        finish(rows, REST, (q_sum[y, rows], qy_full[0, rows], qy_full[1, rows]))

    chunks(tokens, last)
    for one in sent:
        one.wait_send()


def local(gate_pre, up_pre, down_weight, out_grad):
    tokens, units = gate_pre.shape
    feats = out_grad.shape[1]
    first, rest, half = Z_FIRST, units - Z_FIRST, tokens // 2

    def vmem(*shape):
        return pltpu.VMEM(shape, BF16)

    whole = pl.BlockSpec(memory_space=pltpu.VMEM)
    return pl.pallas_call(
        kernel,
        out_shape=(
            jax.ShapeDtypeStruct((tokens, feats), BF16),
            jax.ShapeDtypeStruct((tokens, units), BF16),
            jax.ShapeDtypeStruct((tokens, units), BF16),
        ),
        in_specs=[whole] * 4,
        out_specs=(whole,) * 3,
        scratch_shapes=[
            vmem(16, tokens, units),
            vmem(16, tokens, feats),
            vmem(2, 8, tokens, feats),
            vmem(16, tokens, units),
            vmem(8, tokens, feats),
            vmem(2, 2, tokens, feats),
            vmem(2, 2, half, feats),
            vmem(2, tokens, feats),
            vmem(tokens, feats),
            vmem(2, 4, tokens, first),
            vmem(2, 4, half, first),
            vmem(3, tokens, first),
            vmem(2, tokens, first),
            vmem(2, half, first),
            vmem(2, 4, tokens, rest),
            vmem(2, 4, half, rest),
            vmem(4, tokens, rest),
            vmem(2, tokens, rest),
            vmem(2, half, rest),
            pltpu.SemaphoreType.DMA((len(MESSAGES),)),
            pltpu.SemaphoreType.DMA((len(MESSAGES),)),
        ],
        compiler_params=pltpu.CompilerParams(
            collective_id=0, has_side_effects=True, vmem_limit_bytes=60 * 1024 * 1024
        ),
        cost_estimate=pl.CostEstimate(
            flops=4 * 16 * tokens * units * feats, bytes_accessed=8 * 1024 * 1024, transcendentals=0
        ),
    )(gate_pre, up_pre, down_weight, out_grad)


def solution(mesh):
    return jax.shard_map(
        local,
        mesh=mesh,
        in_specs=(P("col", "row"), P("col", "row"), P("row", "col"), P("row", "col")),
        out_specs=(P("row", "col"), P("col", "row"), P("col", "row")),
        check_vma=False,
    )
```

```python
import jax
import jax.numpy as jnp
from jax import lax
from jax.experimental import pallas as pl
from jax.experimental.pallas import tpu as pltpu
from jax.sharding import PartitionSpec as P

BF16, F32 = jnp.bfloat16, jnp.float32

Z_THEN_Y = 1408
Y_THEN_Z = 1280

ORDER = [
    "gz", "h0.sA", "g0.spread", "h0.sB", "qy.spread", "hz.spread", "g1.spread", "g0.sp", "h0.rp", "h0.rm",
    "qy.rp", "qy.rm", "g1.rm", "g0.sm", "g1.rp", "g1.sm", "h1.sA", "h2.sB", "g1.sf", "hz.rm", "g0.rp",
    "hz.rp", "g0.rm", "qz.spread", "h2.sA", "h2.rm", "g0.sf", "g1.sp", "h1.sB", "h2.rp", "bwd3", "h1.rp",
    "fwd0", "h3.sA", "bwd0", "qz.rm", "qz.rp", "h1.rm", "bwd1", "h3.sB", "rz.far", "op0", "p1.far", "bwd2",
    "p3.far", "fwdP", "fwdO", "rz.nearm", "rz.nearp", "h3.rm", "h3.rp", "p3.near", "opO", "p3.rp", "p3.rm",
    "opP", "o0.start", "fwd3", "rz.rm", "rz.rp", "o0.rm", "p1.rp", "p2.far", "p1.rm", "o0.rp", "op3",
    "o1.start", "p3.here", "pz.far", "p1.near", "p2.rm", "o0.here", "o1.rp", "p2.near", "p2.rp", "p0.far",
    "o1.rm", "o1.here", "oz", "p1.here", "ry.start", "pz.rm", "p2.here", "pz.nearp", "pz.rp", "p0.near",
    "ry.rm", "p0.rm", "p0.rp", "oend", "ry.rp", "pz.nearm", "fin",
]
SEMAPHORES = 128


def kernel(
    gate, up, weight_hbm, cot, out, gate_grad, up_grad,
    weight, hid, cots, part_out, part_grad,
    from_sib, x_full, x_half, x_sum, zl_in,
    y_full, y_half, y_sum, z_full, z_half,
    qz_full, qz_half, q_sum, qy_full, qy_half,
    send_sems, recv_sems, load_sems,
):
    tokens, units = gate.shape
    feats = weight.shape[1]
    half = tokens // 2
    A, B, ALL = pl.ds(0, half), pl.ds(half, half), pl.ds(0, tokens)
    H_FIRST, H_REST = pl.ds(0, Z_THEN_Y), pl.ds(Z_THEN_Y, units - Z_THEN_Y)
    G_FIRST, G_REST = pl.ds(0, Y_THEN_Z), pl.ds(Y_THEN_Z, units - Y_THEN_Z)

    row, col = lax.axis_index("row"), lax.axis_index("col")
    zl, x, core = row // 8, (row // 2) % 4, row % 2
    z, y = col // 4, col % 4
    xs = {d: (x + d) % 4 for d in (0, 1, 2, 3)}
    ys = {d: (y + d) % 4 for d in (0, 1, 2, 3)}
    zs = {d: (z + d) % 4 for d in (0, 1, 2, 3)}

    def at_row(zl_, x_, core_):
        return zl_ * 8 + x_ * 2 + core_

    def at_col(z_, y_):
        return z_ * 4 + y_

    near = {
        "xp": {"row": at_row(zl, xs[1], core)},
        "xm": {"row": at_row(zl, xs[3], core)},
        "zl": {"row": at_row(1 - zl, x, core)},
        "sib": {"row": at_row(zl, x, 1 - core)},
        "yp": {"col": at_col(z, ys[1])},
        "ym": {"col": at_col(z, ys[3])},
        "zp": {"col": at_col(zs[1], y)},
        "zm": {"col": at_col(zs[3], y)},
    }

    numbers, awaited, sent, lands, tasks = {}, set(), [], {}, {}

    def copy(name, src, dst, to):
        number = numbers.setdefault(name, len(numbers))
        return pltpu.make_async_remote_copy(
            src_ref=src,
            dst_ref=dst,
            send_sem=send_sems.at[number],
            recv_sem=recv_sems.at[number],
            device_id=near[to],
            device_id_type=pl.DeviceIdType.MESH,
        )

    def send(name, src, dst, to):
        one = copy(name, src, dst, to)
        one.start()
        sent.append(one)

    def wait(*names):
        for name in names:
            if name not in awaited:
                awaited.add(name)
                copy(name, lands[name], lands[name], "sib").wait_recv()

    def chunks(count, body):
        def step(i, carry):
            body(pl.ds(pl.multiple_of(i * 16, 16), 16))
            return carry

        lax.fori_loop(0, count // 16, step, 0)

    def sum_to(ref, terms):
        lead = (slice(None),) * (len(ref.shape) - 2)

        def body(rows):
            index = lead + (rows,)
            total = terms[0][index].astype(F32)
            for term in terms[1:]:
                total = total + term[index].astype(F32)
            ref[index] = total.astype(BF16)

        chunks(ref.shape[-2], body)

    class Gather:
        def __init__(self, name, axis, block):
            self.name, self.plus, self.minus, self.block = name, axis + "p", axis + "m", block
            lands.update({
                name + "pA": block(3, A), name + "pB": block(3, B), name + "hp": block(2, A),
                name + "mA": block(1, A), name + "mB": block(1, B), name + "hm": block(2, B),
            })
            tasks[name + ".rp"] = self.relay_plus
            tasks[name + ".rm"] = self.relay_minus

        def push(self, what, d, part, to):
            send(self.name + what, self.block(d, part), self.block(d, part), to)

        def spread_a(self):
            self.push("pA", 0, A, self.plus)
            self.push("mA", 0, A, self.minus)

        def spread_b(self):
            self.push("mB", 0, B, self.minus)
            self.push("pB", 0, B, self.plus)

        def spread(self):
            self.push("pA", 0, A, self.plus)
            self.push("mB", 0, B, self.minus)
            self.push("pB", 0, B, self.plus)
            self.push("mA", 0, A, self.minus)

        def relay_plus(self):
            wait(self.name + "pA")
            self.push("hp", 3, A, self.plus)

        def relay_minus(self):
            wait(self.name + "mB")
            self.push("hm", 1, B, self.minus)

        def wait_all(self):
            wait(*[self.name + what for what in ("pA", "pB", "mA", "mB", "hp", "hm")])

    class Scatter:
        def __init__(self, name, axis, part, full, halves):
            self.name, self.plus, self.minus, self.part = name, axis + "p", axis + "m", part
            self.full, self.halves = full, halves
            lead = (slice(None),) * (len(full.shape) - 3)
            self.slot = lambda side, rows: full.at[(side,) + lead + (rows,)]
            lands.update({
                name + "pA": self.slot(0, A), name + "pB": self.slot(0, B), name + "hp": halves.at[0],
                name + "mA": self.slot(1, A), name + "mB": self.slot(1, B), name + "hm": halves.at[1],
            })
            tasks[name + ".far"] = self.far
            tasks[name + ".near"] = self.near
            tasks[name + ".nearp"] = self.near_plus
            tasks[name + ".nearm"] = self.near_minus
            tasks[name + ".rp"] = self.relay_plus
            tasks[name + ".rm"] = self.relay_minus

        def far(self):
            send(self.name + "hp", self.part(2, A), self.halves.at[0], self.plus)
            send(self.name + "hm", self.part(2, B), self.halves.at[1], self.minus)

        def near_plus(self):
            send(self.name + "pB", self.part(1, B), self.slot(0, B), self.plus)

        def near_minus(self):
            send(self.name + "mA", self.part(3, A), self.slot(1, A), self.minus)

        def near(self):
            self.near_plus()
            self.near_minus()

        def relay_plus(self):
            wait(self.name + "hp")
            sum_to(self.part(1, A), (self.part(1, A), self.halves.at[0]))
            send(self.name + "pA", self.part(1, A), self.slot(0, A), self.plus)

        def relay_minus(self):
            wait(self.name + "hm")
            sum_to(self.part(3, B), (self.part(3, B), self.halves.at[1]))
            send(self.name + "mB", self.part(3, B), self.slot(1, B), self.minus)

        def wait_all(self):
            wait(*[self.name + what for what in ("pA", "pB", "mA", "mB")])

    def task(function):
        tasks[function.__name__.replace("_", ".")] = function

    zls = (zl, 1 - zl)
    g = []
    for k in range(2):

        def g_block(d, rows=ALL, core_=core, zl_=zls[k]):
            return cots.at[at_row(zl_, xs[d], core_), rows]

        ring = Gather(f"g{k}", "x", g_block)
        g.append(ring)
        for what, d in (("s", 0), ("sm", 3), ("sp", 1), ("sf", 2)):
            lands[f"g{what}{k}"] = g_block(d, core_=1 - core)

        def g_spread(k=k, ring=ring):
            if k:
                wait("gz")
            ring.spread()
            send(f"gs{k}", ring.block(0), ring.block(0), "sib")

        def g_sib(what, d, needs, k=k, ring=ring):
            wait(*[f"g{k}{need}" for need in needs])
            send(f"g{what}{k}", ring.block(d), ring.block(d), "sib")

        tasks[f"g{k}.spread"] = g_spread
        tasks[f"g{k}.sm"] = lambda f=g_sib: f("sm", 3, ("pA", "pB"))
        tasks[f"g{k}.sp"] = lambda f=g_sib: f("sp", 1, ("mA", "mB"))
        tasks[f"g{k}.sf"] = lambda f=g_sib: f("sf", 2, ("hp", "hm"))
    lands["gz"] = g[1].block(0)

    @task
    def gz():
        send("gz", g[0].block(0), g[0].block(0), "zl")

    def wait_cots():
        wait("gz")
        for k in range(2):
            g[k].wait_all()
            wait(*[f"g{what}{k}" for what in ("s", "sm", "sp", "sf")])
        if "weight" not in awaited:
            awaited.add("weight")
            load_weight.wait()

    hz = Gather("hz", "z", lambda d, rows: hid.at[at_col(zs[d], y), rows, H_FIRST])
    qy = Gather("qy", "y", lambda d, rows: hid.at[at_col(z, ys[d]), rows, H_REST])
    qz = Gather("qz", "z", lambda d, rows: hid.at[pl.ds(zs[d] * 4, 4), rows, H_REST])
    set_z = (zs[0], zs[3], zs[1], zs[2])
    h = [
        Gather(f"h{k}", "y", lambda d, rows, z_=set_z[k]: hid.at[at_col(z_, ys[d]), rows, H_FIRST]) for k in range(4)
    ]
    tasks["hz.spread"] = hz.spread
    tasks["qy.spread"] = qy.spread

    @task
    def qz_spread():
        qy.wait_all()
        qz.spread()

    for k, needs in enumerate((None, ("hzpA", "hzpB"), ("hzmA", "hzmB"), ("hzhp", "hzhm"))):

        def h_first(k=k, needs=needs):
            if needs:
                wait(needs[0])
            h[k].spread_a()

        def h_second(k=k, needs=needs):
            if needs:
                wait(needs[1])
            h[k].spread_b()

        tasks[f"h{k}.sA"], tasks[f"h{k}.sB"] = h_first, h_second

    p = [
        Scatter(
            f"p{k}", "y",
            lambda d, rows, z_=set_z[k]: part_grad.at[at_col(z_, ys[d]), rows, G_FIRST],
            y_full.at[k], y_half.at[k],
        )
        for k in range(4)
    ]
    pz = Scatter("pz", "z", lambda d, rows: y_sum.at[{3: 0, 1: 1, 2: 2}[d], rows], z_full, z_half)
    rz = Scatter("rz", "z", lambda d, rows: part_grad.at[pl.ds(zs[d] * 4, 4), rows, G_REST], qz_full, qz_half)
    ry = Scatter("ry", "y", lambda d, rows: q_sum.at[ys[d], rows], qy_full, qy_half)

    def backward(z_):
        wait_cots()
        four = pl.ds(z_ * 4, 4)

        def tile(start, width):
            left = cots[four].reshape(4 * tokens, feats)
            product = lax.dot_general(
                left, weight[pl.ds(start, width)], (((1,), (1,)), ((), ())), preferred_element_type=F32
            )
            part_grad[four, :, pl.ds(start, width)] = product.astype(BF16).reshape(4, tokens, width)

        def step(i, carry):
            tile(pl.multiple_of(i * 256, 256), 256)
            return carry

        lax.fori_loop(0, units // 256, step, 0)
        if units % 256:
            tile(units // 256 * 256, units % 256)

    for k in range(4):
        tasks[f"bwd{k}"] = lambda k=k: backward(set_z[k])

    def p_here(k):
        p[k].wait_all()
        sum_to(y_sum.at[k - 1], (p[k].part(0, ALL), y_full.at[k, 0], y_full.at[k, 1]))

    for k in range(1, 4):
        tasks[f"p{k}.here"] = lambda k=k: p_here(k)

    @task
    def ry_start():
        rz.wait_all()
        sum_to(q_sum, (rz.part(0, ALL), qz_full.at[0], qz_full.at[1]))
        ry.far()
        ry.near()

    def forward(name, z_):
        four, chips = pl.ds(z_ * 4, 4), pl.ds(z_ * 2, 2)

        def step(i, carry):
            columns = pl.ds(pl.multiple_of(i * 256, 256), 256)
            left = hid[four].reshape(4 * tokens, units)
            product = jnp.dot(left, weight[:, columns], preferred_element_type=F32).astype(BF16)
            for j in range(4):
                part_out[j % 2, z_ * 2 + j // 2, :, columns] = product[j * tokens : (j + 1) * tokens]
            return carry

        lax.fori_loop(0, feats // 256, step, 0)
        lands["od" + name] = from_sib.at[chips]
        send("od" + name, part_out.at[1 - core, chips], from_sib.at[chips], "sib")

    def add_sibling(name, z_):
        chips = pl.ds(z_ * 2, 2)
        wait("od" + name)
        sum_to(part_out.at[core, chips], (part_out.at[core, chips], from_sib.at[chips]))

    pair = z + 1 - 2 * (z % 2)
    other = zs[1] + zs[3] - pair

    @task
    def fwd0():
        qy.wait_all()
        h[0].wait_all()
        forward("0", z)

    def wait_middle():
        wait("hzpA", "hzpB", "hzmA", "hzmB", "qzpA", "qzpB", "qzmA", "qzmB")
        h[1].wait_all()
        h[2].wait_all()

    @task
    def fwdP():
        wait_middle()
        forward("P", pair)

    @task
    def fwdO():
        wait_middle()
        forward("O", other)

    @task
    def fwd3():
        hz.wait_all()
        qz.wait_all()
        h[3].wait_all()
        forward("3", zs[2])

    for name, z_ in (("0", z), ("P", pair), ("O", other), ("3", zs[2])):
        tasks["op" + name] = lambda name=name, z_=z_: add_sibling(name, z_)

    o_zl = (z // 2, 1 - z // 2)
    o = [
        Scatter(
            f"o{m}", "x", lambda d, rows, zl_=o_zl[m]: part_out.at[core, zl_ * 4 + xs[d], rows], x_full.at[m], x_half.at[m]
        )
        for m in range(2)
    ]

    def o_start(m):
        o[m].far()
        o[m].near()

    def o_here(m):
        o[m].wait_all()
        sum_to(x_sum.at[o_zl[m]], (o[m].part(0, ALL), x_full.at[m, 0], x_full.at[m, 1]))

    for m in range(2):
        tasks[f"o{m}.start"] = lambda m=m: o_start(m)
        tasks[f"o{m}.here"] = lambda m=m: o_here(m)
    lands["oz"] = zl_in

    @task
    def oz():
        send("oz", x_sum.at[1 - zl], zl_in, "zl")

    @task
    def oend():
        wait("oz")
        sum_to(out, (x_sum.at[zl], zl_in))

    def finish(rows, columns, terms):
        grad = terms[0].astype(F32)
        for term in terms[1:]:
            grad = grad + term.astype(F32)
        gate_value = gate[rows, columns].astype(F32)
        up_value = up[rows, columns].astype(F32)
        sigma = 1.0 / (1.0 + jnp.exp(-gate_value))
        scaled = grad * sigma
        gate_grad[rows, columns] = (scaled * up_value * (1.0 + gate_value * (1.0 - sigma))).astype(BF16)
        up_grad[rows, columns] = (scaled * gate_value).astype(BF16)

    @task
    def fin():
        p[0].wait_all()
        pz.wait_all()
        ry.wait_all()

        def last(rows):
            here = part_grad[col, rows, G_FIRST]
            finish(rows, G_FIRST, (here, y_full[0, 0, rows], y_full[0, 1, rows], z_full[0, rows], z_full[1, rows]))
            finish(rows, G_REST, (q_sum[y, rows], qy_full[0, rows], qy_full[1, rows]))

        chunks(tokens, last)

    barrier = pltpu.get_barrier_semaphore()
    for to in near.values():
        pl.semaphore_signal(barrier, inc=1, device_id=to, device_id_type=pl.DeviceIdType.MESH)
    load_cot = pltpu.make_async_copy(cot, cots.at[row], load_sems.at[0])
    load_cot.start()
    load_weight = pltpu.make_async_copy(weight_hbm, weight, load_sems.at[1])
    load_weight.start()

    def make_hidden(rows):
        value = gate[rows].astype(F32)
        silu = value / (1.0 + jnp.exp(-value))
        hid[col, rows] = (silu * up[rows].astype(F32)).astype(BF16)

    chunks(tokens, make_hidden)
    load_cot.wait()
    pl.semaphore_wait(barrier, len(near))

    for name in ORDER:
        tasks[name]()
    for one in sent:
        one.wait_send()


def local(gate_pre, up_pre, down_weight, out_grad):
    tokens, units = gate_pre.shape
    feats = out_grad.shape[1]
    half = tokens // 2
    first, rest = Y_THEN_Z, units - Y_THEN_Z

    def vmem(*shape):
        return pltpu.VMEM(shape, BF16)

    whole = pl.BlockSpec(memory_space=pltpu.VMEM)
    outside = pl.BlockSpec(memory_space=pl.ANY)
    return pl.pallas_call(
        kernel,
        out_shape=(
            jax.ShapeDtypeStruct((tokens, feats), BF16),
            jax.ShapeDtypeStruct((tokens, units), BF16),
            jax.ShapeDtypeStruct((tokens, units), BF16),
        ),
        in_specs=[whole, whole, outside, outside],
        out_specs=(whole,) * 3,
        scratch_shapes=[
            vmem(units, feats),
            vmem(16, tokens, units),
            vmem(16, tokens, feats),
            vmem(2, 8, tokens, feats),
            vmem(16, tokens, units),
            vmem(8, tokens, feats),
            vmem(2, 2, tokens, feats),
            vmem(2, 2, half, feats),
            vmem(2, tokens, feats),
            vmem(tokens, feats),
            vmem(4, 2, tokens, first),
            vmem(4, 2, half, first),
            vmem(3, tokens, first),
            vmem(2, tokens, first),
            vmem(2, half, first),
            vmem(2, 4, tokens, rest),
            vmem(2, 4, half, rest),
            vmem(4, tokens, rest),
            vmem(2, tokens, rest),
            vmem(2, half, rest),
            pltpu.SemaphoreType.DMA((SEMAPHORES,)),
            pltpu.SemaphoreType.DMA((SEMAPHORES,)),
            pltpu.SemaphoreType.DMA((2,)),
        ],
        compiler_params=pltpu.CompilerParams(
            collective_id=0, has_side_effects=True, vmem_limit_bytes=60 * 1024 * 1024
        ),
        cost_estimate=pl.CostEstimate(
            flops=4 * 16 * tokens * units * feats, bytes_accessed=8 * 1024 * 1024, transcendentals=0
        ),
    )(gate_pre, up_pre, down_weight, out_grad)


def solution(mesh):
    return jax.shard_map(
        local,
        mesh=mesh,
        in_specs=(P("col", "row"), P("col", "row"), P("row", "col"), P("row", "col")),
        out_specs=(P("row", "col"), P("col", "row"), P("col", "row")),
        check_vma=False,
    )
```

```python
import jax
import jax.numpy as jnp
from jax import lax
from jax.experimental import pallas as pl
from jax.experimental.pallas import tpu as pltpu
from jax.sharding import PartitionSpec as P

BF16, F32 = jnp.bfloat16, jnp.float32

CHUNKS = 4
Z_FIRST = (0,)

ORDER = [
    10, 12, 18, 0, 1, 39, 14, 41, 13, 24, 16, 11,
    42, 40, 5, 101, 30, 15, 45, 102, 36, 25, 43,
    37, 9, 3, 32, 99, 44, 22, 17, 20, 100, 26, 7,
    103, 46, 38, 104, 19, 27, 115, 31, 107, 28,
    116, 2, 21, 8, 108, 105, 106, 117, 34, 6, 47,
    111, 109, 23, 35, 33, 164, 29, 162, 118, 128,
    110, 48, 119, 58, 50, 112, 165, 166, 57, 51,
    113, 163, 175, 56, 127, 4, 52, 126, 97, 96,
    114, 168, 173, 167, 174, 121, 53, 54, 169,
    183, 84, 95, 82, 120, 88, 122, 135, 89, 87,
    139, 137, 182, 90, 75, 76, 181, 141, 71, 143,
    86, 91, 140, 138, 150, 83, 73, 93, 70, 92,
    144, 129, 62, 142, 158, 63, 69, 184, 185, 78,
    149, 176, 148, 177, 74, 79, 77, 55, 49, 156,
    80, 94, 157, 133, 68, 134, 61, 60, 66, 151,
    152, 67, 159, 160, 64, 65, 81, 98, 59, 136,
    186, 72, 161, 85, 188, 187,
]
SEMAPHORES = 256


def kernel(
    gate_hbm, up_hbm, weight_hbm, cot, out, grad,
    gate, up, weight, weight_in, hid_own, hid, hid_set, cots, part_out, from_sib,
    x_full, x_half, x_sum, pair_in, zl_in,
    part_grad, q_in, z_full, z_half, zq_full, zq_half, fy_out, fy_in, grad_t,
    send_sems, recv_sems, load_sems,
):
    tokens, units = gate.shape
    feats = weight.shape[1]
    half, mine = tokens // 2, units // 2
    step_rows = mine // CHUNKS
    A, B, ALL = pl.ds(0, half), pl.ds(half, half), pl.ds(0, tokens)

    row, col = lax.axis_index("row"), lax.axis_index("col")
    zl, x, core = row // 8, (row // 2) % 4, row % 2
    z, y = col // 4, col % 4
    y_pair, y_q = y + 1 - 2 * (y % 2), 3 - y
    kind = (y % 2 + y // 2) % 2
    here, there = y // 2 * 2, 2 - y // 2 * 2
    xs = {d: (x + d) % 4 for d in (0, 1, 2, 3)}
    zs = {d: (z + d) % 4 for d in (0, 1, 2, 3)}

    def at_row(zl_, x_, core_):
        return zl_ * 8 + x_ * 2 + core_

    def at_col(z_, y_):
        return z_ * 4 + y_

    near = {
        "xp": {"row": at_row(zl, xs[1], core)},
        "xm": {"row": at_row(zl, xs[3], core)},
        "zl": {"row": at_row(1 - zl, x, core)},
        "sib": {"row": at_row(zl, x, 1 - core)},
        "pr": {"col": at_col(z, y_pair)},
        "q": {"col": at_col(z, y_q)},
        "zp": {"col": at_col(zs[1], y)},
        "zm": {"col": at_col(zs[3], y)},
    }

    numbers, awaited, sent, lands, tasks = {}, set(), [], {}, {}

    def copy(name, src, dst, to):
        number = numbers.setdefault(name, len(numbers))
        return pltpu.make_async_remote_copy(
            src_ref=src,
            dst_ref=dst,
            send_sem=send_sems.at[number],
            recv_sem=recv_sems.at[number],
            device_id=near[to],
            device_id_type=pl.DeviceIdType.MESH,
        )

    def send(name, src, dst, to):
        one = copy(name, src, dst, to)
        one.start()
        sent.append(one)

    def wait(*names):
        for name in names:
            if name not in awaited:
                awaited.add(name)
                copy(name, lands[name], lands[name], "sib").wait_recv()

    def chunks(count, body):
        def step(i, carry):
            body(pl.ds(pl.multiple_of(i * 16, 16), 16))
            return carry

        lax.fori_loop(0, count // 16, step, 0)

    def sum_to(ref, terms):
        lead = (slice(None),) * (len(ref.shape) - 2)

        def body(rows):
            index = lead + (rows,)
            ref[index] = total_of([term[index] for term in terms]).astype(BF16)

        count, columns = ref.shape[-2:]
        if columns > 128:
            chunks(count, body)
        else:
            for start in range(0, count, 16):
                body(pl.ds(start, 16))

    def total_of(terms):
        result = terms[0].astype(F32)
        for term in terms[1:]:
            result = result + term.astype(F32)
        return result

    class Gather:
        def __init__(self, name, axis, block):
            self.name, self.plus, self.minus, self.block = name, axis + "p", axis + "m", block
            lands.update({
                name + "pA": block(3, A), name + "pB": block(3, B), name + "hp": block(2, A),
                name + "mA": block(1, A), name + "mB": block(1, B), name + "hm": block(2, B),
            })
            tasks[name + ".rp"] = self.relay_plus
            tasks[name + ".rm"] = self.relay_minus

        def push(self, what, d, part, to):
            send(self.name + what, self.block(d, part), self.block(d, part), to)

        def spread_a(self):
            self.push("pA", 0, A, self.plus)
            self.push("mA", 0, A, self.minus)

        def spread_b(self):
            self.push("mB", 0, B, self.minus)
            self.push("pB", 0, B, self.plus)

        def spread(self):
            self.push("pA", 0, A, self.plus)
            self.push("mB", 0, B, self.minus)
            self.push("pB", 0, B, self.plus)
            self.push("mA", 0, A, self.minus)

        def relay_plus(self):
            wait(self.name + "pA")
            self.push("hp", 3, A, self.plus)

        def relay_minus(self):
            wait(self.name + "mB")
            self.push("hm", 1, B, self.minus)

        def wait_all(self):
            wait(*[self.name + what for what in ("pA", "pB", "mA", "mB", "hp", "hm")])

    class Scatter:
        def __init__(self, name, axis, part, slot, halves):
            self.name, self.plus, self.minus, self.part = name, axis + "p", axis + "m", part
            self.slot, self.halves = slot, halves
            lands.update({
                name + "pA": self.slot(0, A), name + "pB": self.slot(0, B), name + "hp": halves(0),
                name + "mA": self.slot(1, A), name + "mB": self.slot(1, B), name + "hm": halves(1),
            })
            tasks[name + ".far"] = self.far
            tasks[name + ".nearp"] = self.near_plus
            tasks[name + ".nearm"] = self.near_minus
            tasks[name + ".rp"] = self.relay_plus
            tasks[name + ".rm"] = self.relay_minus

        def far(self):
            send(self.name + "hp", self.part(2, A), self.halves(0), self.plus)
            send(self.name + "hm", self.part(2, B), self.halves(1), self.minus)

        def near_plus(self):
            send(self.name + "pB", self.part(1, B), self.slot(0, B), self.plus)

        def near_minus(self):
            send(self.name + "mA", self.part(3, A), self.slot(1, A), self.minus)

        def near(self):
            self.near_plus()
            self.near_minus()

        def relay_plus(self):
            wait(self.name + "hp")
            sum_to(self.part(1, A), (self.part(1, A), self.halves(0)))
            send(self.name + "pA", self.part(1, A), self.slot(0, A), self.plus)

        def relay_minus(self):
            wait(self.name + "hm")
            sum_to(self.part(3, B), (self.part(3, B), self.halves(1)))
            send(self.name + "mB", self.part(3, B), self.slot(1, B), self.minus)

        def wait_all(self):
            wait(*[self.name + what for what in ("pA", "pB", "mA", "mB")])

    def task(function):
        tasks[function.__name__.replace("_", ".")] = function

    @task
    def hid_():
        load_gate.wait()
        load_up.wait()
        for u in range(0, units, 128):
            columns = pl.ds(u, 128)
            value = gate[:, columns].astype(F32)
            silu = value / (1.0 + jnp.exp(-value))
            hidden = silu * up[:, columns].astype(F32)
            hid_own[columns] = hidden.T.astype(BF16)
        hid[col] = hid_own[pl.ds(pl.multiple_of(kind * mine, 16), mine)]

    @task
    def e0():
        rows = pl.ds(pl.multiple_of((1 - kind) * mine, 16), mine)
        send("e0", hid_own.at[rows], hid.at[col], "pr")

    lands["e0"] = hid.at[at_col(z, y_pair)]

    def chunk(j):
        return pl.ds(j * step_rows, step_rows)

    columns_of = {"0": pl.ds(0, feats), "a": pl.ds(0, feats // 2), "b": pl.ds(feats // 2, feats // 2)}

    def w_send(j, e):
        if "weight" not in awaited:
            awaited.add("weight")
            load_weight.wait()
        rows = pl.ds(pl.multiple_of((1 - kind) * mine + j * step_rows, 16), step_rows)
        send(f"w{j}{e}", weight.at[rows, columns_of[e]], weight_in.at[chunk(j), columns_of[e]], "pr")

    for j in range(CHUNKS):
        for e in "ab":
            lands[f"w{j}{e}"] = weight_in.at[chunk(j), columns_of[e]]
            tasks[f"w{j}{e}"] = lambda j=j, e=e: w_send(j, e)

    @task
    def c1():
        send("c1", cots.at[0, row], cots.at[1, row], "pr")

    @task
    def c2():
        wait("gz")
        away = at_row(1 - zl, x, core)
        send("c2", cots.at[0, away], cots.at[1, away], "pr")

    lands["c1"] = cots.at[1, row]
    lands["c2"] = cots.at[1, at_row(1 - zl, x, core)]
    zls = (zl, 1 - zl)
    g = {}

    def g_spread(name, ring, needs):
        wait(*needs)
        ring.spread()
        send(name + "s", ring.block(0), ring.block(0), "sib")

    def g_sib(name, ring, what, d, needs):
        wait(*[name + need for need in needs])
        send(name + what, ring.block(d), ring.block(d), "sib")

    @task
    def gz():
        send("gz", cots.at[0, row], cots.at[0, row], "zl")

    lands["gz"] = cots.at[0, at_row(1 - zl, x, core)]

    for i in range(2):
        for k in range(2):

            def g_block(d, rows=ALL, core_=core, i=i, zl_=zls[k]):
                return cots.at[i, at_row(zl_, xs[d], core_), rows]

            name = f"g{i}{k}"
            ring = g[i, k] = Gather(name, "x", g_block)
            for what, d, needs in (
                ("s", 0, ()), ("sm", 3, ("pA", "pB")), ("sp", 1, ("mA", "mB")), ("sf", 2, ("hp", "hm"))
            ):
                lands[name + what] = g_block(d, core_=1 - core)
                if needs:
                    tasks[f"{name}.{what}"] = lambda *a, args=(name, ring, what, d, needs): g_sib(*args)
            needs = ("gz", "c2")[i : i + 1] if k else ("c1",) if i else ()
            tasks[name + ".spread"] = lambda args=(name, ring, needs): g_spread(*args)

    def wait_cots():
        for i in range(2):
            for k in range(2):
                g[i, k].wait_all()
                wait(*[f"g{i}{k}{what}" for what in ("s", "sm", "sp", "sf")])

    def hid_block(z_, part):
        return hid.at[at_col(z_, y if part is A else y_pair)]

    hz = Gather("hz", "z", lambda d, part: hid_block(zs[d], part))
    pair = z + 1 - 2 * (z % 2)
    other = zs[1] + zs[3] - pair
    hid_z = (zs[0], pair, other, zs[2])
    set_z = (zs[0], zs[3], zs[1], zs[2])

    def hz_first():
        hz.spread_a()

    def hz_second():
        wait("e0")
        hz.spread_b()

    tasks["hz.sA"], tasks["hz.sB"] = hz_first, hz_second

    def h_send(k, part, needs):
        wait(*needs)
        block = hid_block(hid_z[k], part)
        send(f"h{k}" + ("A" if part is A else "B"), block, block, "q")

    first_near, second_near = ("hzpA", "hzmA"), ("hzpB", "hzmB")
    arrivals = (((), ("e0",)), (first_near, second_near), (first_near, second_near), (("hzhp",), ("hzhm",)))
    for k, (first, second) in enumerate(arrivals):
        lands[f"h{k}A"] = hid.at[at_col(hid_z[k], y_q)]
        lands[f"h{k}B"] = hid.at[at_col(hid_z[k], 3 - y_pair)]
        tasks[f"h{k}.A"] = lambda k=k, needs=first: h_send(k, A, needs)
        tasks[f"h{k}.B"] = lambda k=k, needs=second: h_send(k, B, needs)

    def q_send(k, j):
        send(f"s{k}{j}", part_grad.at[pl.ds(set_z[k] * 4 + there, 2), chunk(j)], q_in.at[k, :, chunk(j)], "q")

    def backward(k, j):
        wait_cots()
        wait(f"w{j}a", f"w{j}b")
        if "weight" not in awaited:
            awaited.add("weight")
            load_weight.wait()
        four = pl.ds(set_z[k] * 4, 4)
        own = pl.ds(pl.multiple_of(kind * mine + j * step_rows, 16), step_rows)
        total = None
        for i, rows in enumerate((weight[own], weight_in[chunk(j)])):
            right = cots[i, four].reshape(4 * tokens, feats)
            product = lax.dot_general(rows, right, (((1,), (1,)), ((), ())), preferred_element_type=F32)
            total = product if total is None else total + product
        total = total.astype(BF16)
        for b in range(4):
            part_grad[set_z[k] * 4 + b, chunk(j)] = total[:, b * tokens : (b + 1) * tokens]
        if j not in Z_FIRST:
            q_send(k, j)

    def q_add(k, j):
        wait(f"s{k}{j}")
        two = part_grad.at[pl.ds(set_z[k] * 4 + here, 2), chunk(j)]
        sum_to(two, (two, q_in.at[k, :, chunk(j)]))

    def pair_end(j):
        wait(f"s0{j}")
        p_rings[j].wait_all()
        sides = () if j in Z_FIRST else (0, 1)
        own, others = at_col(z, y), at_col(z, y_pair)
        to = pl.multiple_of(kind * mine + j * step_rows, 16)

        for i in range(step_rows // 16):
            rows = pl.ds(j * step_rows + i * 16, 16)
            fy_out[rows] = total_of(
                [part_grad[others, rows], q_in[0, 1 - y % 2, rows]] + [z_full[side, 1, rows] for side in sides]
            ).astype(BF16)
            grad_t[pl.ds(to + i * 16, 16)] = total_of(
                [part_grad[own, rows], q_in[0, y % 2, rows]] + [z_full[side, 0, rows] for side in sides]
            )
        send(f"fy{j}", fy_out.at[chunk(j)], fy_in.at[chunk(j)], "pr")

    def z_first_end(j):
        p_rings[j].wait_all()
        for start, part in ((there, 2), (here, 0)):
            two = part_grad.at[pl.ds(z * 4 + start, 2), chunk(j)]
            sum_to(two, (two, zq_full.at[0, part : part + 2], zq_full.at[1, part : part + 2]))
            if part:
                q_send(0, j)

    p_rings = []
    for j in range(CHUNKS):
        if j in Z_FIRST:

            def part(d, which, j=j):
                return part_grad.at[pl.ds(zs[d] * 4 + (here if which is A else there), 2), chunk(j)]

            def slot(side, which):
                return zq_full.at[side, 0:2] if which is A else zq_full.at[side, 2:4]

            def halves(side):
                return zq_half.at[side]

            tasks[f"sq{j}"] = lambda j=j: z_first_end(j)
        else:

            def part(d, which, j=j):
                return part_grad.at[at_col(zs[d], y if which is A else y_pair), chunk(j)]

            def slot(side, which, j=j):
                return z_full.at[side, 0 if which is A else 1, chunk(j)]

            def halves(side, j=j):
                return z_half.at[side, chunk(j)]

            for k in range(1, 4):
                tasks[f"p{k}{j}"] = lambda k=k, j=j: q_add(k, j)
        p_rings.append(Scatter(f"pz{j}", "z", part, slot, halves))
        for k in range(4):
            lands[f"s{k}{j}"] = q_in.at[k, :, chunk(j)]
            tasks[f"b{k}{j}"] = lambda k=k, j=j: backward(k, j)
        lands[f"fy{j}"] = fy_in.at[chunk(j)]
        tasks[f"fy{j}"] = lambda j=j: pair_end(j)

    def turn(k, y_, needs):
        wait(*needs)
        z_ = hid_z[k]
        rows = pl.ds(pl.multiple_of(y_ * tokens, tokens), tokens)
        for u in range(0, mine, 128):
            width = min(128, mine - u)
            tile = hid[at_col(z_, y_), u : u + width].astype(F32).T
            hid_set[k, rows, u : u + width] = tile.astype(BF16)

    for k, (first, second) in enumerate(arrivals):
        for what, y_, needs in (
            ("a", y, first), ("b", y_pair, second),
            ("c", y_q, (f"h{k}A",)), ("d", 3 - y_pair, (f"h{k}B",)),
        ):
            tasks[f"t{k}{what}"] = lambda args=(k, y_, needs): turn(*args)

    def forward(e, s, k, z_):
        chips, i, where = pl.ds(z_ * 2, 2), 0 if e == "0" else 1, columns_of[e]
        name = f"f{e}{s}"
        if i:
            wait(*[f"w{j}{e}" for j in range(CHUNKS)])
        elif "weight" not in awaited:
            awaited.add("weight")
            load_weight.wait()
        own = pl.ds(pl.multiple_of(kind * mine, 16), mine)

        def step(n, carry):
            columns = pl.ds(pl.multiple_of(where.start + n * 256, 256), 256)
            right = weight_in[:, columns] if i else weight[own, columns]
            product = jnp.dot(hid_set[k], right, preferred_element_type=F32).astype(BF16)
            for b in range(4):
                part_out[i, b % 2, z_ * 2 + b // 2, :, columns] = product[b * tokens : (b + 1) * tokens]
            return carry

        lax.fori_loop(0, where.size // 256, step, 0)
        lands[name] = from_sib.at[i, chips, :, where]
        send(name, part_out.at[i, 1 - core, chips, :, where], from_sib.at[i, chips, :, where], "sib")

    def add_sibling(e, s, z_):
        chips, i, where = pl.ds(z_ * 2, 2), 0 if e == "0" else 1, columns_of[e]
        wait(f"f{e}{s}")
        two = part_out.at[i, core, chips, :, where]
        sum_to(two, (two, from_sib.at[i, chips, :, where]))

    o_zl = (z // 2, 1 - z // 2)

    def o_start(ring):
        ring.far()
        ring.near()

    def o_here(e, m, ring):
        i, where = 0 if e == "0" else 1, columns_of[e]
        ring.wait_all()
        sum_to(
            x_sum.at[i, o_zl[m], :, where],
            (ring.part(0, ALL), x_full.at[i, m, 0, :, where], x_full.at[i, m, 1, :, where]),
        )

    def o_pair(e, m):
        where = columns_of[e]
        send(f"oy{e}{m}", x_sum.at[1, o_zl[m], :, where], pair_in.at[o_zl[m], :, where], "pr")

    def o_cross(e):
        where = columns_of[e]
        wait(f"oy{e}0", f"oy{e}1")
        away = x_sum.at[0, 1 - zl, :, where]
        sum_to(away, (away, pair_in.at[1 - zl, :, where]))
        send(f"oz{e}", away, zl_in.at[:, where], "zl")

    for e, where in columns_of.items():
        i = 0 if e == "0" else 1
        for k, (name, z_) in enumerate(zip("0PO3", hid_z)):
            tasks[f"f{e}{name}"] = lambda args=(e, name, k, z_): forward(*args)
            tasks[f"op{e}{name}"] = lambda args=(e, name, z_): add_sibling(*args)
        for m in range(2):
            ring = Scatter(
                f"o{e}{m}", "x",
                lambda d, rows, i=i, zl_=o_zl[m], where=where: part_out.at[i, core, zl_ * 4 + xs[d], rows, where],
                lambda side, rows, i=i, m=m, where=where: x_full.at[i, m, side, rows, where],
                lambda side, i=i, m=m, where=where: x_half.at[i, m, side, :, where],
            )
            tasks[f"o{e}{m}.start"] = lambda ring=ring: o_start(ring)
            tasks[f"o{e}{m}.here"] = lambda args=(e, m, ring): o_here(*args)
            if i:
                lands[f"oy{e}{m}"] = pair_in.at[o_zl[m], :, where]
                tasks[f"oy{e}{m}"] = lambda args=(e, m): o_pair(*args)
        if i:
            lands[f"oz{e}"] = zl_in.at[:, where]
            tasks[f"oz{e}"] = lambda e=e: o_cross(e)

    @task
    def oend():
        wait("oza", "ozb")
        sum_to(out, (x_sum.at[0, zl], pair_in.at[zl], zl_in))

    @task
    def fin():
        wait(*[f"fy{j}" for j in range(CHUNKS)])
        others = pl.multiple_of((1 - kind) * mine, 16)

        grad_t[pl.ds(others, mine)] = fy_in[...].astype(F32)
        for u in range(0, units, 128):
            grad[:, u : u + 128] = grad_t[pl.ds(u, 128)].T

    barrier = pltpu.get_barrier_semaphore()
    for to in near.values():
        pl.semaphore_signal(barrier, inc=1, device_id=to, device_id_type=pl.DeviceIdType.MESH)
    load_cot = pltpu.make_async_copy(cot, cots.at[0, row], load_sems.at[0])
    load_cot.start()
    load_gate = pltpu.make_async_copy(gate_hbm, gate, load_sems.at[2])
    load_gate.start()
    load_up = pltpu.make_async_copy(up_hbm, up, load_sems.at[3])
    load_up.start()
    load_weight = pltpu.make_async_copy(weight_hbm, weight, load_sems.at[1])
    load_weight.start()
    load_cot.wait()
    pl.semaphore_wait(barrier, len(near))

    steps = list(tasks.values())
    for number in ORDER:
        steps[number]()
    for one in sent:
        one.wait_send()


def finish(gate, up, grad, summed, out, gate_grad, up_grad):
    value = gate[...].astype(F32)
    sigma = 1.0 / (1.0 + jnp.exp(-value))
    scaled = grad[...] * sigma
    gate_grad[...] = (scaled * up[...].astype(F32) * (1.0 + value * (1.0 - sigma))).astype(BF16)
    up_grad[...] = (scaled * value).astype(BF16)
    out[...] = summed[...]


def local(gate_pre, up_pre, down_weight, out_grad):
    tokens, units = gate_pre.shape
    feats = out_grad.shape[1]
    half, mine = tokens // 2, units // 2

    def vmem(*shape):
        return pltpu.VMEM(shape, BF16)

    whole = pl.BlockSpec(memory_space=pltpu.VMEM)
    outside = pl.BlockSpec(memory_space=pl.ANY)
    summed, grad = pl.pallas_call(
        kernel,
        out_shape=(
            jax.ShapeDtypeStruct((tokens, feats), BF16),
            jax.ShapeDtypeStruct((tokens, units), F32),
        ),
        in_specs=[outside] * 4,
        out_specs=(whole,) * 2,
        scratch_shapes=[
            vmem(tokens, units),
            vmem(tokens, units),
            vmem(units, feats),
            vmem(mine, feats),
            vmem(units, tokens),
            vmem(16, mine, tokens),
            vmem(4, 4 * tokens, mine),
            vmem(2, 16, tokens, feats),
            vmem(2, 2, 8, tokens, feats),
            vmem(2, 8, tokens, feats),
            vmem(2, 2, 2, tokens, feats),
            vmem(2, 2, 2, half, feats),
            vmem(2, 2, tokens, feats),
            vmem(2, tokens, feats),
            vmem(tokens, feats),
            vmem(16, mine, tokens),
            vmem(4, 2, mine, tokens),
            vmem(2, 2, mine, tokens),
            vmem(2, mine, tokens),
            vmem(2, 4, mine // CHUNKS, tokens),
            vmem(2, 2, mine // CHUNKS, tokens),
            vmem(mine, tokens),
            vmem(mine, tokens),
            pltpu.VMEM((units, tokens), F32),
            pltpu.SemaphoreType.DMA((SEMAPHORES,)),
            pltpu.SemaphoreType.DMA((SEMAPHORES,)),
            pltpu.SemaphoreType.DMA((4,)),
        ],
        compiler_params=pltpu.CompilerParams(
            collective_id=0, has_side_effects=True, vmem_limit_bytes=60 * 1024 * 1024
        ),
        cost_estimate=pl.CostEstimate(
            flops=4 * 16 * tokens * units * feats, bytes_accessed=8 * 1024 * 1024, transcendentals=0
        ),
    )(gate_pre, up_pre, down_weight, out_grad)
    by_units, by_feats = (pl.BlockSpec((tokens // 2, n), lambda i: (i, 0)) for n in (units, feats))
    return pl.pallas_call(
        finish,
        grid=(2,),
        out_shape=(
            jax.ShapeDtypeStruct((tokens, feats), BF16),
            jax.ShapeDtypeStruct((tokens, units), BF16),
            jax.ShapeDtypeStruct((tokens, units), BF16),
        ),
        in_specs=[by_units, by_units, by_units, by_feats],
        out_specs=(by_feats, by_units, by_units),
    )(gate_pre, up_pre, grad, summed)


def solution(mesh):
    return jax.shard_map(
        local,
        mesh=mesh,
        in_specs=(P("col", "row"), P("col", "row"), P("row", "col"), P("row", "col")),
        out_specs=(P("row", "col"), P("col", "row"), P("col", "row")),
        check_vma=False,
    )
```

```python
import jax
import jax.numpy as jnp
from jax import lax
from jax.experimental import pallas as pl
from jax.experimental.pallas import tpu as pltpu
from jax.sharding import PartitionSpec as P

BF16, F32 = jnp.bfloat16, jnp.float32

CHUNKS = (144,176,176,176,160)
Z_FIRST = (0,)

ORDER = [
    12, 14, 20, 0, 1, 43, 41, 15, 16, 114, 13, 32,
    44, 42, 26, 7, 19, 5, 47, 45, 117, 38, 28, 23,
    39, 22, 27, 21, 116, 11, 122, 46, 124, 18, 34,
    9, 33, 40, 115, 48, 3, 36, 202, 180, 29, 118,
    2, 203, 119, 120, 10, 8, 17, 4, 24, 31, 6,
    181, 123, 35, 30, 121, 204, 182, 25, 49, 205,
    215, 126, 183, 193, 37, 157, 155, 50, 125,
    159, 206, 60, 52, 214, 158, 59, 53, 128, 184,
    112, 207, 156, 168, 213, 127, 58, 54, 111,
    160, 129, 161, 99, 103, 104, 110, 56, 55, 208,
    167, 166, 162, 176, 73, 102, 105, 98, 97, 90,
    91, 107, 71, 209, 222, 101, 106, 130, 132,
    174, 175, 108, 64, 65, 134, 136, 86, 131, 133,
    143, 89, 88, 93, 92, 72, 135, 95, 137, 151,
    94, 169, 85, 170, 62, 186, 77, 78, 141, 142,
    220, 84, 177, 221, 69, 178, 63, 66, 96, 68,
    149, 67, 150, 57, 51, 144, 145, 185, 187, 200,
    191, 76, 75, 80, 81, 79, 70, 152, 153, 192,
    82, 83, 223, 216, 198, 199, 100, 179, 109, 74,
    194, 61, 201, 154, 87, 113, 225, 224,
]
SEMAPHORES = 256


def kernel(
    gate_hbm, up_hbm, weight_hbm, cot, out, grad,
    gate, up, weight, weight_in, hid_own, hid, hid_set, cots, part_out, from_sib,
    x_full, x_half, x_sum, pair_in, zl_in,
    part_grad, q_in, z_full, z_half, zq_full, zq_half, fy_out, fy_in, grad_t,
    send_sems, recv_sems, load_sems,
):
    tokens, units = gate.shape
    feats = weight.shape[1]
    half, mine = tokens // 2, units // 2
    A, B, ALL = pl.ds(0, half), pl.ds(half, half), pl.ds(0, tokens)

    row, col = lax.axis_index("row"), lax.axis_index("col")
    zl, x, core = row // 8, (row // 2) % 4, row % 2
    z, y = col // 4, col % 4
    y_pair, y_q = y + 1 - 2 * (y % 2), 3 - y
    kind = (y % 2 + y // 2) % 2
    here, there = y // 2 * 2, 2 - y // 2 * 2
    xs = {d: (x + d) % 4 for d in (0, 1, 2, 3)}
    zs = {d: (z + d) % 4 for d in (0, 1, 2, 3)}

    def at_row(zl_, x_, core_):
        return zl_ * 8 + x_ * 2 + core_

    def at_col(z_, y_):
        return z_ * 4 + y_

    near = {
        "xp": {"row": at_row(zl, xs[1], core)},
        "xm": {"row": at_row(zl, xs[3], core)},
        "zl": {"row": at_row(1 - zl, x, core)},
        "sib": {"row": at_row(zl, x, 1 - core)},
        "pr": {"col": at_col(z, y_pair)},
        "q": {"col": at_col(z, y_q)},
        "zp": {"col": at_col(zs[1], y)},
        "zm": {"col": at_col(zs[3], y)},
    }

    numbers, awaited, sent, lands, tasks = {}, set(), [], {}, {}

    def copy(name, src, dst, to):
        number = numbers.setdefault(name, len(numbers))
        return pltpu.make_async_remote_copy(
            src_ref=src,
            dst_ref=dst,
            send_sem=send_sems.at[number],
            recv_sem=recv_sems.at[number],
            device_id=near[to],
            device_id_type=pl.DeviceIdType.MESH,
        )

    def send(name, src, dst, to):
        one = copy(name, src, dst, to)
        one.start()
        sent.append(one)

    def wait(*names):
        for name in names:
            if name not in awaited:
                awaited.add(name)
                copy(name, lands[name], lands[name], "sib").wait_recv()

    def chunks(count, body):
        def step(i, carry):
            body(pl.ds(pl.multiple_of(i * 16, 16), 16))
            return carry

        lax.fori_loop(0, count // 16, step, 0)

    def sum_to(ref, terms):
        lead = (slice(None),) * (len(ref.shape) - 2)

        def body(rows):
            index = lead + (rows,)
            ref[index] = total_of([term[index] for term in terms]).astype(BF16)

        count, columns = ref.shape[-2:]
        if columns > 128:
            chunks(count, body)
        else:
            for start in range(0, count, 16):
                body(pl.ds(start, 16))

    def total_of(terms):
        result = terms[0].astype(F32)
        for term in terms[1:]:
            result = result + term.astype(F32)
        return result

    class Gather:
        def __init__(self, name, axis, block):
            self.name, self.plus, self.minus, self.block = name, axis + "p", axis + "m", block
            lands.update({
                name + "pA": block(3, A), name + "pB": block(3, B), name + "hp": block(2, A),
                name + "mA": block(1, A), name + "mB": block(1, B), name + "hm": block(2, B),
            })
            tasks[name + ".rp"] = self.relay_plus
            tasks[name + ".rm"] = self.relay_minus

        def push(self, what, d, part, to):
            send(self.name + what, self.block(d, part), self.block(d, part), to)

        def spread_a(self):
            self.push("pA", 0, A, self.plus)
            self.push("mA", 0, A, self.minus)

        def spread_b(self):
            self.push("mB", 0, B, self.minus)
            self.push("pB", 0, B, self.plus)

        def spread(self):
            self.push("pA", 0, A, self.plus)
            self.push("mB", 0, B, self.minus)
            self.push("pB", 0, B, self.plus)
            self.push("mA", 0, A, self.minus)

        def relay_plus(self):
            wait(self.name + "pA")
            self.push("hp", 3, A, self.plus)

        def relay_minus(self):
            wait(self.name + "mB")
            self.push("hm", 1, B, self.minus)

        def wait_all(self):
            wait(*[self.name + what for what in ("pA", "pB", "mA", "mB", "hp", "hm")])

    class Scatter:
        def __init__(self, name, axis, part, slot, halves):
            self.name, self.plus, self.minus, self.part = name, axis + "p", axis + "m", part
            self.slot, self.halves = slot, halves
            lands.update({
                name + "pA": self.slot(0, A), name + "pB": self.slot(0, B), name + "hp": halves(0),
                name + "mA": self.slot(1, A), name + "mB": self.slot(1, B), name + "hm": halves(1),
            })
            tasks[name + ".far"] = self.far
            tasks[name + ".nearp"] = self.near_plus
            tasks[name + ".nearm"] = self.near_minus
            tasks[name + ".rp"] = self.relay_plus
            tasks[name + ".rm"] = self.relay_minus

        def far(self):
            send(self.name + "hp", self.part(2, A), self.halves(0), self.plus)
            send(self.name + "hm", self.part(2, B), self.halves(1), self.minus)

        def near_plus(self):
            send(self.name + "pB", self.part(1, B), self.slot(0, B), self.plus)

        def near_minus(self):
            send(self.name + "mA", self.part(3, A), self.slot(1, A), self.minus)

        def near(self):
            self.near_plus()
            self.near_minus()

        def relay_plus(self):
            wait(self.name + "hp")
            sum_to(self.part(1, A), (self.part(1, A), self.halves(0)))
            send(self.name + "pA", self.part(1, A), self.slot(0, A), self.plus)

        def relay_minus(self):
            wait(self.name + "hm")
            sum_to(self.part(3, B), (self.part(3, B), self.halves(1)))
            send(self.name + "mB", self.part(3, B), self.slot(1, B), self.minus)

        def wait_all(self):
            wait(*[self.name + what for what in ("pA", "pB", "mA", "mB")])

    def task(function):
        tasks[function.__name__.replace("_", ".")] = function

    @task
    def hid_():
        load_gate.wait()
        load_up.wait()
        for u in range(0, units, 128):
            columns = pl.ds(u, 128)
            value = gate[:, columns].astype(F32)
            silu = value / (1.0 + jnp.exp(-value))
            hidden = silu * up[:, columns].astype(F32)
            hid_own[columns] = hidden.T.astype(BF16)
        hid[col] = hid_own[pl.ds(pl.multiple_of(kind * mine, 16), mine)]

    @task
    def e0():
        rows = pl.ds(pl.multiple_of((1 - kind) * mine, 16), mine)
        send("e0", hid_own.at[rows], hid.at[col], "pr")

    lands["e0"] = hid.at[at_col(z, y_pair)]

    def chunk(j):
        return pl.ds(sum(CHUNKS[:j]), CHUNKS[j])

    columns_of = {e: pl.ds(n % 2 * (feats // 2), feats // 2) for n, e in enumerate("abcd")}

    def w_send(j, e):
        if "weight" not in awaited:
            awaited.add("weight")
            load_weight.wait()
        rows = pl.ds(pl.multiple_of((1 - kind) * mine + sum(CHUNKS[:j]), 16), CHUNKS[j])
        send(f"w{j}{e}", weight.at[rows, columns_of[e]], weight_in.at[chunk(j), columns_of[e]], "pr")

    for j in range(len(CHUNKS)):
        for e in "ab":
            lands[f"w{j}{e}"] = weight_in.at[chunk(j), columns_of[e]]
            tasks[f"w{j}{e}"] = lambda j=j, e=e: w_send(j, e)

    @task
    def c1():
        send("c1", cots.at[0, row], cots.at[1, row], "pr")

    @task
    def c2():
        wait("gz")
        away = at_row(1 - zl, x, core)
        send("c2", cots.at[0, away], cots.at[1, away], "pr")

    lands["c1"] = cots.at[1, row]
    lands["c2"] = cots.at[1, at_row(1 - zl, x, core)]
    zls = (zl, 1 - zl)
    g = {}

    def g_spread(name, ring, needs):
        wait(*needs)
        ring.spread()
        send(name + "s", ring.block(0), ring.block(0), "sib")

    def g_sib(name, ring, what, d, needs):
        wait(*[name + need for need in needs])
        send(name + what, ring.block(d), ring.block(d), "sib")

    @task
    def gz():
        send("gz", cots.at[0, row], cots.at[0, row], "zl")

    lands["gz"] = cots.at[0, at_row(1 - zl, x, core)]

    for i in range(2):
        for k in range(2):

            def g_block(d, rows=ALL, core_=core, i=i, zl_=zls[k]):
                return cots.at[i, at_row(zl_, xs[d], core_), rows]

            name = f"g{i}{k}"
            ring = g[i, k] = Gather(name, "x", g_block)
            for what, d, needs in (
                ("s", 0, ()), ("sm", 3, ("pA", "pB")), ("sp", 1, ("mA", "mB")), ("sf", 2, ("hp", "hm"))
            ):
                lands[name + what] = g_block(d, core_=1 - core)
                if needs:
                    tasks[f"{name}.{what}"] = lambda *a, args=(name, ring, what, d, needs): g_sib(*args)
            needs = ("gz", "c2")[i : i + 1] if k else ("c1",) if i else ()
            tasks[name + ".spread"] = lambda args=(name, ring, needs): g_spread(*args)

    def wait_cots():
        for i in range(2):
            for k in range(2):
                g[i, k].wait_all()
                wait(*[f"g{i}{k}{what}" for what in ("s", "sm", "sp", "sf")])

    def hid_block(z_, part):
        return hid.at[at_col(z_, y if part is A else y_pair)]

    hz = Gather("hz", "z", lambda d, part: hid_block(zs[d], part))
    pair = z + 1 - 2 * (z % 2)
    other = zs[1] + zs[3] - pair
    hid_z = (zs[0], pair, other, zs[2])
    set_z = (zs[0], zs[3], zs[1], zs[2])

    def hz_first():
        hz.spread_a()

    def hz_second():
        wait("e0")
        hz.spread_b()

    tasks["hz.sA"], tasks["hz.sB"] = hz_first, hz_second

    def h_send(k, part, needs):
        wait(*needs)
        block = hid_block(hid_z[k], part)
        send(f"h{k}" + ("A" if part is A else "B"), block, block, "q")

    first_near, second_near = ("hzpA", "hzmA"), ("hzpB", "hzmB")
    arrivals = (((), ("e0",)), (first_near, second_near), (first_near, second_near), (("hzhp",), ("hzhm",)))
    for k, (first, second) in enumerate(arrivals):
        lands[f"h{k}A"] = hid.at[at_col(hid_z[k], y_q)]
        lands[f"h{k}B"] = hid.at[at_col(hid_z[k], 3 - y_pair)]
        tasks[f"h{k}.A"] = lambda k=k, needs=first: h_send(k, A, needs)
        tasks[f"h{k}.B"] = lambda k=k, needs=second: h_send(k, B, needs)

    def q_send(k, j):
        send(f"s{k}{j}", part_grad.at[pl.ds(set_z[k] * 4 + there, 2), chunk(j)], q_in.at[k, :, chunk(j)], "q")

    def backward(k, j):
        wait_cots()
        wait(f"w{j}a", f"w{j}b")
        if "weight" not in awaited:
            awaited.add("weight")
            load_weight.wait()
        four = pl.ds(set_z[k] * 4, 4)
        own = pl.ds(pl.multiple_of(kind * mine + sum(CHUNKS[:j]), 16), CHUNKS[j])
        total = None
        for i, rows in enumerate((weight[own], weight_in[chunk(j)])):
            right = cots[i, four].reshape(4 * tokens, feats)
            product = lax.dot_general(rows, right, (((1,), (1,)), ((), ())), preferred_element_type=F32)
            total = product if total is None else total + product
        total = total.astype(BF16)
        for b in range(4):
            part_grad[set_z[k] * 4 + b, chunk(j)] = total[:, b * tokens : (b + 1) * tokens]
        if j not in Z_FIRST:
            q_send(k, j)

    def q_add(k, j):
        wait(f"s{k}{j}")
        two = part_grad.at[pl.ds(set_z[k] * 4 + here, 2), chunk(j)]
        sum_to(two, (two, q_in.at[k, :, chunk(j)]))

    def pair_end(j):
        wait(f"s0{j}")
        p_rings[j].wait_all()
        sides = () if j in Z_FIRST else (0, 1)
        own, others = at_col(z, y), at_col(z, y_pair)
        to = pl.multiple_of(kind * mine + sum(CHUNKS[:j]), 16)

        for i in range(CHUNKS[j] // 16):
            rows = pl.ds(sum(CHUNKS[:j]) + i * 16, 16)
            fy_out[rows] = total_of(
                [part_grad[others, rows], q_in[0, 1 - y % 2, rows]] + [z_full[side, 1, rows] for side in sides]
            ).astype(BF16)
            grad_t[pl.ds(to + i * 16, 16)] = total_of(
                [part_grad[own, rows], q_in[0, y % 2, rows]] + [z_full[side, 0, rows] for side in sides]
            )
        send(f"fy{j}", fy_out.at[chunk(j)], fy_in.at[chunk(j)], "pr")

    def z_first_end(j):
        p_rings[j].wait_all()
        for start, part in ((there, 2), (here, 0)):
            two = part_grad.at[pl.ds(z * 4 + start, 2), chunk(j)]
            sum_to(two, (two, zq_full.at[0, part : part + 2], zq_full.at[1, part : part + 2]))
            if part:
                q_send(0, j)

    p_rings = []
    for j in range(len(CHUNKS)):
        if j in Z_FIRST:

            def part(d, which, j=j):
                return part_grad.at[pl.ds(zs[d] * 4 + (here if which is A else there), 2), chunk(j)]

            def slot(side, which):
                return zq_full.at[side, 0:2] if which is A else zq_full.at[side, 2:4]

            def halves(side):
                return zq_half.at[side]

            tasks[f"sq{j}"] = lambda j=j: z_first_end(j)
        else:

            def part(d, which, j=j):
                return part_grad.at[at_col(zs[d], y if which is A else y_pair), chunk(j)]

            def slot(side, which, j=j):
                return z_full.at[side, 0 if which is A else 1, chunk(j)]

            def halves(side, j=j):
                return z_half.at[side, chunk(j)]

            for k in range(1, 4):
                tasks[f"p{k}{j}"] = lambda k=k, j=j: q_add(k, j)
        p_rings.append(Scatter(f"pz{j}", "z", part, slot, halves))
        for k in range(4):
            lands[f"s{k}{j}"] = q_in.at[k, :, chunk(j)]
            tasks[f"b{k}{j}"] = lambda k=k, j=j: backward(k, j)
        lands[f"fy{j}"] = fy_in.at[chunk(j)]
        tasks[f"fy{j}"] = lambda j=j: pair_end(j)

    def turn(k, y_, needs):
        wait(*needs)
        z_ = hid_z[k]
        rows = pl.ds(pl.multiple_of(y_ * tokens, tokens), tokens)
        for u in range(0, mine, 128):
            width = min(128, mine - u)
            tile = hid[at_col(z_, y_), u : u + width].astype(F32).T
            hid_set[k, rows, u : u + width] = tile.astype(BF16)

    for k, (first, second) in enumerate(arrivals):
        for what, y_, needs in (
            ("a", y, first), ("b", y_pair, second),
            ("c", y_q, (f"h{k}A",)), ("d", 3 - y_pair, (f"h{k}B",)),
        ):
            tasks[f"t{k}{what}"] = lambda args=(k, y_, needs): turn(*args)

    def forward(e, s, k, z_):
        chips, i, where = pl.ds(z_ * 2, 2), 1 if e in "ab" else 0, columns_of[e]
        name = f"f{e}{s}"
        if i:
            wait(*[f"w{j}{e}" for j in range(len(CHUNKS))])
        elif "weight" not in awaited:
            awaited.add("weight")
            load_weight.wait()
        own = pl.ds(pl.multiple_of(kind * mine, 16), mine)

        right = weight_in[:, where] if i else weight[own, where]
        product = jnp.dot(hid_set[k], right, preferred_element_type=F32).astype(BF16)
        for b in range(4):
            part_out[i, b % 2, z_ * 2 + b // 2, :, where] = product[b * tokens : (b + 1) * tokens]
        lands[name] = from_sib.at[i, chips, :, where]
        send(name, part_out.at[i, 1 - core, chips, :, where], from_sib.at[i, chips, :, where], "sib")

    def add_sibling(e, s, z_):
        chips, i, where = pl.ds(z_ * 2, 2), 1 if e in "ab" else 0, columns_of[e]
        wait(f"f{e}{s}")
        two = part_out.at[i, core, chips, :, where]
        sum_to(two, (two, from_sib.at[i, chips, :, where]))

    o_zl = (z // 2, 1 - z // 2)

    def o_start(ring):
        ring.far()
        ring.near()

    def o_here(e, m, ring):
        i, where = 1 if e in "ab" else 0, columns_of[e]
        ring.wait_all()
        sum_to(
            x_sum.at[i, o_zl[m], :, where],
            (ring.part(0, ALL), x_full.at[i, m, 0, :, where], x_full.at[i, m, 1, :, where]),
        )

    def o_pair(e, m):
        where = columns_of[e]
        send(f"oy{e}{m}", x_sum.at[1, o_zl[m], :, where], pair_in.at[o_zl[m], :, where], "pr")

    def o_cross(e):
        where = columns_of[e]
        wait(f"oy{e}0", f"oy{e}1")
        away = x_sum.at[0, 1 - zl, :, where]
        sum_to(away, (away, pair_in.at[1 - zl, :, where]))
        send(f"oz{e}", away, zl_in.at[:, where], "zl")

    for e, where in columns_of.items():
        i = 1 if e in "ab" else 0
        for k, (name, z_) in enumerate(zip("0PO3", hid_z)):
            tasks[f"f{e}{name}"] = lambda args=(e, name, k, z_): forward(*args)
            tasks[f"op{e}{name}"] = lambda args=(e, name, z_): add_sibling(*args)
        for m in range(2):
            ring = Scatter(
                f"o{e}{m}", "x",
                lambda d, rows, i=i, zl_=o_zl[m], where=where: part_out.at[i, core, zl_ * 4 + xs[d], rows, where],
                lambda side, rows, i=i, m=m, where=where: x_full.at[i, m, side, rows, where],
                lambda side, i=i, m=m, where=where: x_half.at[i, m, side, :, where],
            )
            tasks[f"o{e}{m}.start"] = lambda ring=ring: o_start(ring)
            tasks[f"o{e}{m}.here"] = lambda args=(e, m, ring): o_here(*args)
            if i:
                lands[f"oy{e}{m}"] = pair_in.at[o_zl[m], :, where]
                tasks[f"oy{e}{m}"] = lambda args=(e, m): o_pair(*args)
        if i:
            lands[f"oz{e}"] = zl_in.at[:, where]
            tasks[f"oz{e}"] = lambda e=e: o_cross(e)

    @task
    def oend():
        wait("oza", "ozb")
        sum_to(out, (x_sum.at[0, zl], pair_in.at[zl], zl_in))

    @task
    def fin():
        wait(*[f"fy{j}" for j in range(len(CHUNKS))])
        others = pl.multiple_of((1 - kind) * mine, 16)

        grad_t[pl.ds(others, mine)] = fy_in[...].astype(F32)
        for u in range(0, units, 128):
            grad[:, u : u + 128] = grad_t[pl.ds(u, 128)].T

    barrier = pltpu.get_barrier_semaphore()
    for to in near.values():
        pl.semaphore_signal(barrier, inc=1, device_id=to, device_id_type=pl.DeviceIdType.MESH)
    load_cot = pltpu.make_async_copy(cot, cots.at[0, row], load_sems.at[0])
    load_cot.start()
    load_gate = pltpu.make_async_copy(gate_hbm, gate, load_sems.at[2])
    load_gate.start()
    load_up = pltpu.make_async_copy(up_hbm, up, load_sems.at[3])
    load_up.start()
    load_weight = pltpu.make_async_copy(weight_hbm, weight, load_sems.at[1])
    load_weight.start()
    load_cot.wait()
    pl.semaphore_wait(barrier, len(near))

    steps = list(tasks.values())
    for number in ORDER:
        steps[number]()
    for one in sent:
        one.wait_send()


def finish(gate, up, grad, summed, out, gate_grad, up_grad):
    value = gate[...].astype(F32)
    sigma = 1.0 / (1.0 + jnp.exp(-value))
    scaled = grad[...] * sigma
    gate_grad[...] = (scaled * up[...].astype(F32) * (1.0 + value * (1.0 - sigma))).astype(BF16)
    up_grad[...] = (scaled * value).astype(BF16)
    out[...] = summed[...]


def local(gate_pre, up_pre, down_weight, out_grad):
    tokens, units = gate_pre.shape
    feats = out_grad.shape[1]
    half, mine = tokens // 2, units // 2

    def vmem(*shape):
        return pltpu.VMEM(shape, BF16)

    whole = pl.BlockSpec(memory_space=pltpu.VMEM)
    outside = pl.BlockSpec(memory_space=pl.ANY)
    summed, grad = pl.pallas_call(
        kernel,
        out_shape=(
            jax.ShapeDtypeStruct((tokens, feats), BF16),
            jax.ShapeDtypeStruct((tokens, units), F32),
        ),
        in_specs=[outside] * 4,
        out_specs=(whole,) * 2,
        scratch_shapes=[
            vmem(tokens, units),
            vmem(tokens, units),
            vmem(units, feats),
            vmem(mine, feats),
            vmem(units, tokens),
            vmem(16, mine, tokens),
            vmem(4, 4 * tokens, mine),
            vmem(2, 16, tokens, feats),
            vmem(2, 2, 8, tokens, feats),
            vmem(2, 8, tokens, feats),
            vmem(2, 2, 2, tokens, feats),
            vmem(2, 2, 2, half, feats),
            vmem(2, 2, tokens, feats),
            vmem(2, tokens, feats),
            vmem(tokens, feats),
            vmem(16, mine, tokens),
            vmem(4, 2, mine, tokens),
            vmem(2, 2, mine, tokens),
            vmem(2, mine, tokens),
            vmem(2, 4, sum(CHUNKS[j] for j in Z_FIRST), tokens),
            vmem(2, 2, sum(CHUNKS[j] for j in Z_FIRST), tokens),
            vmem(mine, tokens),
            vmem(mine, tokens),
            pltpu.VMEM((units, tokens), F32),
            pltpu.SemaphoreType.DMA((SEMAPHORES,)),
            pltpu.SemaphoreType.DMA((SEMAPHORES,)),
            pltpu.SemaphoreType.DMA((4,)),
        ],
        compiler_params=pltpu.CompilerParams(
            collective_id=0, has_side_effects=True, vmem_limit_bytes=60 * 1024 * 1024
        ),
        cost_estimate=pl.CostEstimate(
            flops=4 * 16 * tokens * units * feats, bytes_accessed=8 * 1024 * 1024, transcendentals=0
        ),
    )(gate_pre, up_pre, down_weight, out_grad)
    by_units, by_feats = (pl.BlockSpec((tokens // 2, n), lambda i: (i, 0)) for n in (units, feats))
    return pl.pallas_call(
        finish,
        grid=(2,),
        out_shape=(
            jax.ShapeDtypeStruct((tokens, feats), BF16),
            jax.ShapeDtypeStruct((tokens, units), BF16),
            jax.ShapeDtypeStruct((tokens, units), BF16),
        ),
        in_specs=[by_units, by_units, by_units, by_feats],
        out_specs=(by_feats, by_units, by_units),
    )(gate_pre, up_pre, grad, summed)


def solution(mesh):
    return jax.shard_map(
        local,
        mesh=mesh,
        in_specs=(P("col", "row"), P("col", "row"), P("row", "col"), P("row", "col")),
        out_specs=(P("row", "col"), P("col", "row"), P("col", "row")),
        check_vma=False,
    )
```

```python
import jax
import jax.numpy as jnp
from jax import lax
from jax.experimental import pallas as pl
from jax.experimental.pallas import tpu as pltpu
from jax.sharding import PartitionSpec as P

BF16, F32 = jnp.bfloat16, jnp.float32

CHUNKS = (144,176,176,176,160)
Z_FIRST = (0,)

ORDER = [
    12, 14, 20, 0, 1, 43, 41, 15, 16, 114, 13, 32,
    44, 42, 26, 7, 19, 5, 47, 45, 117, 38, 28, 23,
    39, 22, 27, 21, 116, 11, 122, 46, 124, 18, 34,
    9, 33, 40, 115, 48, 3, 36, 202, 180, 29, 118,
    2, 203, 119, 120, 10, 8, 17, 4, 24, 31, 6,
    181, 123, 35, 30, 121, 204, 182, 25, 49, 205,
    215, 126, 183, 193, 37, 157, 155, 50, 125,
    159, 206, 60, 52, 214, 158, 59, 53, 128, 184,
    112, 207, 156, 168, 213, 127, 58, 54, 111,
    160, 129, 161, 99, 103, 104, 110, 56, 55, 208,
    167, 166, 162, 176, 73, 102, 105, 98, 97, 90,
    91, 107, 71, 209, 222, 101, 106, 130, 132,
    174, 175, 108, 64, 65, 134, 136, 86, 131, 133,
    143, 89, 88, 93, 92, 72, 135, 95, 137, 151,
    94, 169, 85, 170, 62, 186, 77, 78, 141, 142,
    220, 84, 177, 221, 69, 178, 63, 66, 96, 68,
    149, 67, 150, 57, 51, 144, 145, 185, 187, 200,
    191, 76, 75, 80, 81, 79, 70, 152, 153, 192,
    82, 83, 223, 216, 198, 199, 100, 179, 109, 74,
    194, 61, 201, 154, 87, 113, 225, 224,
]
SEMAPHORES = 256
PATIENCE = {"sib": 12, "xp": 40, "xm": 40, "q": 50, "zp": 60, "zm": 60, "zl": 60, "pr": 140}


def kernel(
    gate_hbm, up_hbm, weight_hbm, cot, out, grad,
    gate, up, weight, weight_in, hid_own, hid, hid_set, cots, part_out, from_sib,
    x_full, x_half, x_sum, pair_in, zl_in,
    part_grad, q_in, z_full, z_half, zq_full, zq_half, fy_out, fy_in, grad_t,
    send_sems, recv_sems, load_sems,
):
    tokens, units = gate.shape
    feats = weight.shape[1]
    half, mine = tokens // 2, units // 2
    A, B, ALL = pl.ds(0, half), pl.ds(half, half), pl.ds(0, tokens)

    row, col = lax.axis_index("row"), lax.axis_index("col")
    zl, x, core = row // 8, (row // 2) % 4, row % 2
    z, y = col // 4, col % 4
    y_pair, y_q = y + 1 - 2 * (y % 2), 3 - y
    kind = (y % 2 + y // 2) % 2
    here, there = y // 2 * 2, 2 - y // 2 * 2
    xs = {d: (x + d) % 4 for d in (0, 1, 2, 3)}
    zs = {d: (z + d) % 4 for d in (0, 1, 2, 3)}

    def at_row(zl_, x_, core_):
        return zl_ * 8 + x_ * 2 + core_

    def at_col(z_, y_):
        return z_ * 4 + y_

    near = {
        "xp": {"row": at_row(zl, xs[1], core)},
        "xm": {"row": at_row(zl, xs[3], core)},
        "zl": {"row": at_row(1 - zl, x, core)},
        "sib": {"row": at_row(zl, x, 1 - core)},
        "pr": {"col": at_col(z, y_pair)},
        "q": {"col": at_col(z, y_q)},
        "zp": {"col": at_col(zs[1], y)},
        "zm": {"col": at_col(zs[3], y)},
    }

    numbers, awaited, sent, lands, tasks = {}, set(), [], {}, {}
    counter = [0]

    def copy(name, src, dst, to):
        number = numbers.setdefault(name, len(numbers))
        return pltpu.make_async_remote_copy(
            src_ref=src,
            dst_ref=dst,
            send_sem=send_sems.at[number],
            recv_sem=recv_sems.at[number],
            device_id=near[to],
            device_id_type=pl.DeviceIdType.MESH,
        )

    def send(name, src, dst, to):
        one = copy(name, src, dst, to)
        one.start()
        sent.append((one, counter[0] + PATIENCE[to]))
        counter[0] += 1

    def wait(*names):
        for name in names:
            if name not in awaited:
                awaited.add(name)
                copy(name, lands[name], lands[name], "sib").wait_recv()

    def chunks(count, body):
        def step(i, carry):
            body(pl.ds(pl.multiple_of(i * 16, 16), 16))
            return carry

        lax.fori_loop(0, count // 16, step, 0)

    def sum_to(ref, terms):
        lead = (slice(None),) * (len(ref.shape) - 2)

        def body(rows):
            index = lead + (rows,)
            ref[index] = total_of([term[index] for term in terms]).astype(BF16)

        count, columns = ref.shape[-2:]
        if columns > 128:
            chunks(count, body)
        else:
            for start in range(0, count, 16):
                body(pl.ds(start, 16))

    def total_of(terms):
        result = terms[0].astype(F32)
        for term in terms[1:]:
            result = result + term.astype(F32)
        return result

    class Gather:
        def __init__(self, name, axis, block):
            self.name, self.plus, self.minus, self.block = name, axis + "p", axis + "m", block
            lands.update({
                name + "pA": block(3, A), name + "pB": block(3, B), name + "hp": block(2, A),
                name + "mA": block(1, A), name + "mB": block(1, B), name + "hm": block(2, B),
            })
            tasks[name + ".rp"] = self.relay_plus
            tasks[name + ".rm"] = self.relay_minus

        def push(self, what, d, part, to):
            send(self.name + what, self.block(d, part), self.block(d, part), to)

        def spread_a(self):
            self.push("pA", 0, A, self.plus)
            self.push("mA", 0, A, self.minus)

        def spread_b(self):
            self.push("mB", 0, B, self.minus)
            self.push("pB", 0, B, self.plus)

        def spread(self):
            self.push("pA", 0, A, self.plus)
            self.push("mB", 0, B, self.minus)
            self.push("pB", 0, B, self.plus)
            self.push("mA", 0, A, self.minus)

        def relay_plus(self):
            wait(self.name + "pA")
            self.push("hp", 3, A, self.plus)

        def relay_minus(self):
            wait(self.name + "mB")
            self.push("hm", 1, B, self.minus)

        def wait_all(self):
            wait(*[self.name + what for what in ("pA", "pB", "mA", "mB", "hp", "hm")])

    class Scatter:
        def __init__(self, name, axis, part, slot, halves):
            self.name, self.plus, self.minus, self.part = name, axis + "p", axis + "m", part
            self.slot, self.halves = slot, halves
            lands.update({
                name + "pA": self.slot(0, A), name + "pB": self.slot(0, B), name + "hp": halves(0),
                name + "mA": self.slot(1, A), name + "mB": self.slot(1, B), name + "hm": halves(1),
            })
            tasks[name + ".far"] = self.far
            tasks[name + ".nearp"] = self.near_plus
            tasks[name + ".nearm"] = self.near_minus
            tasks[name + ".rp"] = self.relay_plus
            tasks[name + ".rm"] = self.relay_minus

        def far(self):
            send(self.name + "hp", self.part(2, A), self.halves(0), self.plus)
            send(self.name + "hm", self.part(2, B), self.halves(1), self.minus)

        def near_plus(self):
            send(self.name + "pB", self.part(1, B), self.slot(0, B), self.plus)

        def near_minus(self):
            send(self.name + "mA", self.part(3, A), self.slot(1, A), self.minus)

        def near(self):
            self.near_plus()
            self.near_minus()

        def relay_plus(self):
            wait(self.name + "hp")
            sum_to(self.part(1, A), (self.part(1, A), self.halves(0)))
            send(self.name + "pA", self.part(1, A), self.slot(0, A), self.plus)

        def relay_minus(self):
            wait(self.name + "hm")
            sum_to(self.part(3, B), (self.part(3, B), self.halves(1)))
            send(self.name + "mB", self.part(3, B), self.slot(1, B), self.minus)

        def wait_all(self):
            wait(*[self.name + what for what in ("pA", "pB", "mA", "mB")])

    def task(function):
        tasks[function.__name__.replace("_", ".")] = function

    @task
    def hid_():
        load_gate.wait()
        load_up.wait()
        for u in range(0, units, 128):
            columns = pl.ds(u, 128)
            value = gate[:, columns].astype(F32)
            silu = value / (1.0 + jnp.exp(-value))
            hidden = silu * up[:, columns].astype(F32)
            hid_own[columns] = hidden.T.astype(BF16)
        hid[col] = hid_own[pl.ds(pl.multiple_of(kind * mine, 16), mine)]

    @task
    def e0():
        rows = pl.ds(pl.multiple_of((1 - kind) * mine, 16), mine)
        send("e0", hid_own.at[rows], hid.at[col], "pr")

    lands["e0"] = hid.at[at_col(z, y_pair)]

    def chunk(j):
        return pl.ds(sum(CHUNKS[:j]), CHUNKS[j])

    columns_of = {e: pl.ds(n % 2 * (feats // 2), feats // 2) for n, e in enumerate("abcd")}

    def w_send(j, e):
        if "weight" not in awaited:
            awaited.add("weight")
            load_weight.wait()
        rows = pl.ds(pl.multiple_of((1 - kind) * mine + sum(CHUNKS[:j]), 16), CHUNKS[j])
        send(f"w{j}{e}", weight.at[rows, columns_of[e]], weight_in.at[chunk(j), columns_of[e]], "pr")

    for j in range(len(CHUNKS)):
        for e in "ab":
            lands[f"w{j}{e}"] = weight_in.at[chunk(j), columns_of[e]]
            tasks[f"w{j}{e}"] = lambda j=j, e=e: w_send(j, e)

    @task
    def c1():
        send("c1", cots.at[0, row], cots.at[1, row], "pr")

    @task
    def c2():
        wait("gz")
        away = at_row(1 - zl, x, core)
        send("c2", cots.at[0, away], cots.at[1, away], "pr")

    lands["c1"] = cots.at[1, row]
    lands["c2"] = cots.at[1, at_row(1 - zl, x, core)]
    zls = (zl, 1 - zl)
    g = {}

    def g_spread(name, ring, needs):
        wait(*needs)
        ring.spread()
        send(name + "s", ring.block(0), ring.block(0), "sib")

    def g_sib(name, ring, what, d, needs):
        wait(*[name + need for need in needs])
        send(name + what, ring.block(d), ring.block(d), "sib")

    @task
    def gz():
        send("gz", cots.at[0, row], cots.at[0, row], "zl")

    lands["gz"] = cots.at[0, at_row(1 - zl, x, core)]

    for i in range(2):
        for k in range(2):

            def g_block(d, rows=ALL, core_=core, i=i, zl_=zls[k]):
                return cots.at[i, at_row(zl_, xs[d], core_), rows]

            name = f"g{i}{k}"
            ring = g[i, k] = Gather(name, "x", g_block)
            for what, d, needs in (
                ("s", 0, ()), ("sm", 3, ("pA", "pB")), ("sp", 1, ("mA", "mB")), ("sf", 2, ("hp", "hm"))
            ):
                lands[name + what] = g_block(d, core_=1 - core)
                if needs:
                    tasks[f"{name}.{what}"] = lambda *a, args=(name, ring, what, d, needs): g_sib(*args)
            needs = ("gz", "c2")[i : i + 1] if k else ("c1",) if i else ()
            tasks[name + ".spread"] = lambda args=(name, ring, needs): g_spread(*args)

    def wait_cots():
        for i in range(2):
            for k in range(2):
                g[i, k].wait_all()
                wait(*[f"g{i}{k}{what}" for what in ("s", "sm", "sp", "sf")])

    def hid_block(z_, part):
        return hid.at[at_col(z_, y if part is A else y_pair)]

    hz = Gather("hz", "z", lambda d, part: hid_block(zs[d], part))
    pair = z + 1 - 2 * (z % 2)
    other = zs[1] + zs[3] - pair
    hid_z = (zs[0], pair, other, zs[2])
    set_z = (zs[0], zs[3], zs[1], zs[2])

    def hz_first():
        hz.spread_a()

    def hz_second():
        wait("e0")
        hz.spread_b()

    tasks["hz.sA"], tasks["hz.sB"] = hz_first, hz_second

    def h_send(k, part, needs):
        wait(*needs)
        block = hid_block(hid_z[k], part)
        send(f"h{k}" + ("A" if part is A else "B"), block, block, "q")

    first_near, second_near = ("hzpA", "hzmA"), ("hzpB", "hzmB")
    arrivals = (((), ("e0",)), (first_near, second_near), (first_near, second_near), (("hzhp",), ("hzhm",)))
    for k, (first, second) in enumerate(arrivals):
        lands[f"h{k}A"] = hid.at[at_col(hid_z[k], y_q)]
        lands[f"h{k}B"] = hid.at[at_col(hid_z[k], 3 - y_pair)]
        tasks[f"h{k}.A"] = lambda k=k, needs=first: h_send(k, A, needs)
        tasks[f"h{k}.B"] = lambda k=k, needs=second: h_send(k, B, needs)

    def q_send(k, j):
        send(f"s{k}{j}", part_grad.at[pl.ds(set_z[k] * 4 + there, 2), chunk(j)], q_in.at[k, :, chunk(j)], "q")

    def backward(k, j):
        wait_cots()
        wait(f"w{j}a", f"w{j}b")
        if "weight" not in awaited:
            awaited.add("weight")
            load_weight.wait()
        four = pl.ds(set_z[k] * 4, 4)
        own = pl.ds(pl.multiple_of(kind * mine + sum(CHUNKS[:j]), 16), CHUNKS[j])
        total = None
        for i, rows in enumerate((weight[own], weight_in[chunk(j)])):
            right = cots[i, four].reshape(4 * tokens, feats)
            product = lax.dot_general(rows, right, (((1,), (1,)), ((), ())), preferred_element_type=F32)
            total = product if total is None else total + product
        total = total.astype(BF16)
        for b in range(4):
            part_grad[set_z[k] * 4 + b, chunk(j)] = total[:, b * tokens : (b + 1) * tokens]
        if j not in Z_FIRST:
            q_send(k, j)

    def q_add(k, j):
        wait(f"s{k}{j}")
        two = part_grad.at[pl.ds(set_z[k] * 4 + here, 2), chunk(j)]
        sum_to(two, (two, q_in.at[k, :, chunk(j)]))

    def pair_end(j):
        wait(f"s0{j}")
        p_rings[j].wait_all()
        sides = () if j in Z_FIRST else (0, 1)
        own, others = at_col(z, y), at_col(z, y_pair)
        to = pl.multiple_of(kind * mine + sum(CHUNKS[:j]), 16)

        for i in range(CHUNKS[j] // 16):
            rows = pl.ds(sum(CHUNKS[:j]) + i * 16, 16)
            fy_out[rows] = total_of(
                [part_grad[others, rows], q_in[0, 1 - y % 2, rows]] + [z_full[side, 1, rows] for side in sides]
            ).astype(BF16)
            grad_t[pl.ds(to + i * 16, 16)] = total_of(
                [part_grad[own, rows], q_in[0, y % 2, rows]] + [z_full[side, 0, rows] for side in sides]
            )
        send(f"fy{j}", fy_out.at[chunk(j)], fy_in.at[chunk(j)], "pr")

    def z_first_end(j):
        p_rings[j].wait_all()
        for start, part in ((there, 2), (here, 0)):
            two = part_grad.at[pl.ds(z * 4 + start, 2), chunk(j)]
            sum_to(two, (two, zq_full.at[0, part : part + 2], zq_full.at[1, part : part + 2]))
            if part:
                q_send(0, j)

    p_rings = []
    for j in range(len(CHUNKS)):
        if j in Z_FIRST:

            def part(d, which, j=j):
                return part_grad.at[pl.ds(zs[d] * 4 + (here if which is A else there), 2), chunk(j)]

            def slot(side, which):
                return zq_full.at[side, 0:2] if which is A else zq_full.at[side, 2:4]

            def halves(side):
                return zq_half.at[side]

            tasks[f"sq{j}"] = lambda j=j: z_first_end(j)
        else:

            def part(d, which, j=j):
                return part_grad.at[at_col(zs[d], y if which is A else y_pair), chunk(j)]

            def slot(side, which, j=j):
                return z_full.at[side, 0 if which is A else 1, chunk(j)]

            def halves(side, j=j):
                return z_half.at[side, chunk(j)]

            for k in range(1, 4):
                tasks[f"p{k}{j}"] = lambda k=k, j=j: q_add(k, j)
        p_rings.append(Scatter(f"pz{j}", "z", part, slot, halves))
        for k in range(4):
            lands[f"s{k}{j}"] = q_in.at[k, :, chunk(j)]
            tasks[f"b{k}{j}"] = lambda k=k, j=j: backward(k, j)
        lands[f"fy{j}"] = fy_in.at[chunk(j)]
        tasks[f"fy{j}"] = lambda j=j: pair_end(j)

    def turn(k, y_, needs):
        wait(*needs)
        z_ = hid_z[k]
        rows = pl.ds(pl.multiple_of(y_ * tokens, tokens), tokens)
        for u in range(0, mine, 128):
            width = min(128, mine - u)
            tile = hid[at_col(z_, y_), u : u + width].astype(F32).T
            hid_set[k, rows, u : u + width] = tile.astype(BF16)

    for k, (first, second) in enumerate(arrivals):
        for what, y_, needs in (
            ("a", y, first), ("b", y_pair, second),
            ("c", y_q, (f"h{k}A",)), ("d", 3 - y_pair, (f"h{k}B",)),
        ):
            tasks[f"t{k}{what}"] = lambda args=(k, y_, needs): turn(*args)

    def forward(e, s, k, z_):
        chips, i, where = pl.ds(z_ * 2, 2), 1 if e in "ab" else 0, columns_of[e]
        name = f"f{e}{s}"
        if i:
            wait(*[f"w{j}{e}" for j in range(len(CHUNKS))])
        elif "weight" not in awaited:
            awaited.add("weight")
            load_weight.wait()
        own = pl.ds(pl.multiple_of(kind * mine, 16), mine)

        right = weight_in[:, where] if i else weight[own, where]
        product = jnp.dot(hid_set[k], right, preferred_element_type=F32).astype(BF16)
        for b in range(4):
            part_out[i, b % 2, z_ * 2 + b // 2, :, where] = product[b * tokens : (b + 1) * tokens]
        lands[name] = from_sib.at[i, chips, :, where]
        send(name, part_out.at[i, 1 - core, chips, :, where], from_sib.at[i, chips, :, where], "sib")

    def add_sibling(e, s, z_):
        chips, i, where = pl.ds(z_ * 2, 2), 1 if e in "ab" else 0, columns_of[e]
        wait(f"f{e}{s}")
        two = part_out.at[i, core, chips, :, where]
        sum_to(two, (two, from_sib.at[i, chips, :, where]))

    o_zl = (z // 2, 1 - z // 2)

    def o_start(ring):
        ring.far()
        ring.near()

    def o_here(e, m, ring):
        i, where = 1 if e in "ab" else 0, columns_of[e]
        ring.wait_all()
        sum_to(
            x_sum.at[i, o_zl[m], :, where],
            (ring.part(0, ALL), x_full.at[i, m, 0, :, where], x_full.at[i, m, 1, :, where]),
        )

    def o_pair(e, m):
        where = columns_of[e]
        send(f"oy{e}{m}", x_sum.at[1, o_zl[m], :, where], pair_in.at[o_zl[m], :, where], "pr")

    def o_cross(e):
        where = columns_of[e]
        wait(f"oy{e}0", f"oy{e}1")
        away = x_sum.at[0, 1 - zl, :, where]
        sum_to(away, (away, pair_in.at[1 - zl, :, where]))
        send(f"oz{e}", away, zl_in.at[:, where], "zl")

    for e, where in columns_of.items():
        i = 1 if e in "ab" else 0
        for k, (name, z_) in enumerate(zip("0PO3", hid_z)):
            tasks[f"f{e}{name}"] = lambda args=(e, name, k, z_): forward(*args)
            tasks[f"op{e}{name}"] = lambda args=(e, name, z_): add_sibling(*args)
        for m in range(2):
            ring = Scatter(
                f"o{e}{m}", "x",
                lambda d, rows, i=i, zl_=o_zl[m], where=where: part_out.at[i, core, zl_ * 4 + xs[d], rows, where],
                lambda side, rows, i=i, m=m, where=where: x_full.at[i, m, side, rows, where],
                lambda side, i=i, m=m, where=where: x_half.at[i, m, side, :, where],
            )
            tasks[f"o{e}{m}.start"] = lambda ring=ring: o_start(ring)
            tasks[f"o{e}{m}.here"] = lambda args=(e, m, ring): o_here(*args)
            if i:
                lands[f"oy{e}{m}"] = pair_in.at[o_zl[m], :, where]
                tasks[f"oy{e}{m}"] = lambda args=(e, m): o_pair(*args)
        if i:
            lands[f"oz{e}"] = zl_in.at[:, where]
            tasks[f"oz{e}"] = lambda e=e: o_cross(e)

    @task
    def oend():
        wait("oza", "ozb")
        sum_to(out, (x_sum.at[0, zl], pair_in.at[zl], zl_in))

    @task
    def fin():
        wait(*[f"fy{j}" for j in range(len(CHUNKS))])
        others = pl.multiple_of((1 - kind) * mine, 16)

        grad_t[pl.ds(others, mine)] = fy_in[...].astype(F32)
        for u in range(0, units, 128):
            grad[:, u : u + 128] = grad_t[pl.ds(u, 128)].T

    barrier = pltpu.get_barrier_semaphore()
    for to in near.values():
        pl.semaphore_signal(barrier, inc=1, device_id=to, device_id_type=pl.DeviceIdType.MESH)
    load_cot = pltpu.make_async_copy(cot, cots.at[0, row], load_sems.at[0])
    load_cot.start()
    load_gate = pltpu.make_async_copy(gate_hbm, gate, load_sems.at[2])
    load_gate.start()
    load_up = pltpu.make_async_copy(up_hbm, up, load_sems.at[3])
    load_up.start()
    load_weight = pltpu.make_async_copy(weight_hbm, weight, load_sems.at[1])
    load_weight.start()
    load_cot.wait()
    pl.semaphore_wait(barrier, len(near))

    steps = list(tasks.values())
    for number in ORDER:
        steps[number]()
        for one, due in sent:
            if due <= counter[0]:
                one.wait_send()
        sent[:] = [entry for entry in sent if entry[1] > counter[0]]
    for one, _ in sent:
        one.wait_send()


def finish(gate, up, grad, summed, out, gate_grad, up_grad):
    value = gate[...].astype(F32)
    sigma = 1.0 / (1.0 + jnp.exp(-value))
    scaled = grad[...] * sigma
    gate_grad[...] = (scaled * up[...].astype(F32) * (1.0 + value * (1.0 - sigma))).astype(BF16)
    up_grad[...] = (scaled * value).astype(BF16)
    out[...] = summed[...]


def local(gate_pre, up_pre, down_weight, out_grad):
    tokens, units = gate_pre.shape
    feats = out_grad.shape[1]
    half, mine = tokens // 2, units // 2

    def vmem(*shape):
        return pltpu.VMEM(shape, BF16)

    whole = pl.BlockSpec(memory_space=pltpu.VMEM)
    outside = pl.BlockSpec(memory_space=pl.ANY)
    summed, grad = pl.pallas_call(
        kernel,
        out_shape=(
            jax.ShapeDtypeStruct((tokens, feats), BF16),
            jax.ShapeDtypeStruct((tokens, units), F32),
        ),
        in_specs=[outside] * 4,
        out_specs=(whole,) * 2,
        scratch_shapes=[
            vmem(tokens, units),
            vmem(tokens, units),
            vmem(units, feats),
            vmem(mine, feats),
            vmem(units, tokens),
            vmem(16, mine, tokens),
            vmem(4, 4 * tokens, mine),
            vmem(2, 16, tokens, feats),
            vmem(2, 2, 8, tokens, feats),
            vmem(2, 8, tokens, feats),
            vmem(2, 2, 2, tokens, feats),
            vmem(2, 2, 2, half, feats),
            vmem(2, 2, tokens, feats),
            vmem(2, tokens, feats),
            vmem(tokens, feats),
            vmem(16, mine, tokens),
            vmem(4, 2, mine, tokens),
            vmem(2, 2, mine, tokens),
            vmem(2, mine, tokens),
            vmem(2, 4, sum(CHUNKS[j] for j in Z_FIRST), tokens),
            vmem(2, 2, sum(CHUNKS[j] for j in Z_FIRST), tokens),
            vmem(mine, tokens),
            vmem(mine, tokens),
            pltpu.VMEM((units, tokens), F32),
            pltpu.SemaphoreType.DMA((SEMAPHORES,)),
            pltpu.SemaphoreType.DMA((SEMAPHORES,)),
            pltpu.SemaphoreType.DMA((4,)),
        ],
        compiler_params=pltpu.CompilerParams(
            collective_id=0, has_side_effects=True, vmem_limit_bytes=60 * 1024 * 1024
        ),
        cost_estimate=pl.CostEstimate(
            flops=4 * 16 * tokens * units * feats, bytes_accessed=8 * 1024 * 1024, transcendentals=0
        ),
    )(gate_pre, up_pre, down_weight, out_grad)
    by_units, by_feats = (pl.BlockSpec((tokens // 2, n), lambda i: (i, 0)) for n in (units, feats))
    return pl.pallas_call(
        finish,
        grid=(2,),
        out_shape=(
            jax.ShapeDtypeStruct((tokens, feats), BF16),
            jax.ShapeDtypeStruct((tokens, units), BF16),
            jax.ShapeDtypeStruct((tokens, units), BF16),
        ),
        in_specs=[by_units, by_units, by_units, by_feats],
        out_specs=(by_feats, by_units, by_units),
    )(gate_pre, up_pre, grad, summed)


def solution(mesh):
    return jax.shard_map(
        local,
        mesh=mesh,
        in_specs=(P("col", "row"), P("col", "row"), P("row", "col"), P("row", "col")),
        out_specs=(P("row", "col"), P("col", "row"), P("col", "row")),
        check_vma=False,
    )
```
